32 devices in a mesh: dom: 16 (over z, x, core), kv: 2 (over y).
Axes of the slice: x: 2, y: 2, z: 4, core: 2. Of those that a mesh axis runs over, the one named last changes fastest.
Arguments:
- positions: float32 [3, 8192], P(None, ('dom', 'kv')), may hold values from 0 to 60
- features: bfloat16 [8192, 128], P(('dom', 'kv')), may hold values from -6 to 6
- nbr_index: int32 [8192, 64], P(('dom', 'kv')), may hold values from 0 to 1023
- nbr_count: int32 [8192], P(('dom', 'kv')), may hold values from 16 to 64
- nbr_dist: float32 [8192, 64], P(('dom', 'kv')), may hold values from 0.8 to 5
- halo_lists: int32 [16, 2, 256], P('dom'), may hold values from 0 to 511
- wave_vectors: float32 [3, 2048], replicated, may hold values from -1.2566371 to 1.2566371, as said below
- w_charge_first: bfloat16 [128, 16], replicated, may hold values from -0.5 to 0.5
- w_long_first: float32 [16, 128], replicated, may hold values from -1.5 to 1.5
- w_value: bfloat16 [128, 128], replicated, may hold values from -0.5 to 0.5
- w_filter: float32 [16, 128], replicated, may hold values from -1.5 to 1.5
- w_charge_second: bfloat16 [128, 16], replicated, may hold values from -0.5 to 0.5
- w_long_second: float32 [16, 128], replicated, may hold values from -1.5 to 1.5
Outputs:
- features_out: bfloat16 [8192, 128], P(('dom', 'kv'))
- forces: float32 [3, 8192], P(None, ('dom', 'kv'))
The draws below stay inside these ranges and needn't reach their ends.
Inputs may be any that keep to these rules, and one draw needn't show every extreme that they name: `nbr_index`: rows of the atom's own domain table. `nbr_count`: slots at or past the count are padding. `halo_lists`: rows among the domain's own 512 atoms; repeats may occur. `wave_vectors`: the columns are 2 pi n / 60 for 2048 distinct nonzero integer vectors n of smallest length, no two equal or opposite, in no particular order.
All inputs are finite; a program needn't handle non-finite values.
Results may differ from the reference program's by a relative error of at most 0.0054.
Values may be sent and summed in bfloat16 or wider, within the bound.
A program may use at most 64 MiB of HBM per device.

```python
import math
import jax
import jax.numpy as jnp
from jax import lax

HID = 128
CHAN = 16
KVEC = 2048
NEIGH = 64
NRBF = 16
DOMS = 16
DOM_ATOMS = 512
HALO = 256
ATOMS = 8192


def draw_wave_vectors(key, part):
    reach = 12
    side = 2 * reach + 1
    flat = jnp.arange(side * side * side, dtype=jnp.int32)
    first = flat // (side * side) - reach
    second = flat // side % side - reach
    third = flat % side - reach
    upper = (first > 0) | (first == 0) & (second > 0) | (first == 0) & (second == 0) & (third > 0)
    sq_len = first * first + second * second + third * third
    order_key = jax.random.fold_in(key, 11)
    sign_key = jax.random.fold_in(key, 23)
    place_key = jax.random.fold_in(key, 37)
    tie_break = jax.random.permutation(order_key, side * side * side).astype(jnp.int32)
    scores = jnp.where(upper, sq_len * 32768 + tie_break, 1073741823)
    chosen = jnp.argsort(scores, stable=True)[:KVEC]
    integer_vecs = jnp.stack([first[chosen], second[chosen], third[chosen]], axis=0)
    signs = jax.random.randint(sign_key, (KVEC,), 0, 2).astype(jnp.int32) * 2 - 1
    integer_vecs = integer_vecs * signs[None, :]
    placed = jax.random.permutation(place_key, KVEC)
    integer_vecs = integer_vecs[:, placed]
    return integer_vecs.astype(jnp.float32) * jnp.float32(2.0 * math.pi / 60.0)


def set_ends(values, key, least, top_value):
    longest = values.shape.index(max(values.shape))
    spots = []
    for shift in (0, 1):
        where = [jax.random.randint(jax.random.fold_in(key, axis), (), 0, length) for axis, length in enumerate(values.shape)]
        where[longest] = (where[longest] + shift) % values.shape[longest]
        spots.append(tuple(where))
    return values.at[spots[0]].set(least).at[spots[1]].set(top_value)


def block_scale(key, dims, cuts, least, top_value):
    loudness = 1.0
    for dim, shards_of in cuts:
        draws = jax.random.uniform(jax.random.fold_in(jax.random.fold_in(key, 6), dim), (shards_of,), jnp.float32, least / len(cuts), top_value / len(cuts))
        loudness = loudness * jnp.repeat(jnp.exp(draws), dims[dim] // shards_of).reshape((-1,) + (1,) * (len(dims) - 1 - dim))
    return loudness


def noise(own_key, dims, scale, bound, shards=(), kind=jnp.bfloat16):
    level = block_scale(own_key, dims, shards, -0.22, 0.18) if shards else 1.0
    array = jax.random.normal(own_key, dims, jnp.float32) * scale * level
    return jnp.minimum(jnp.maximum(array, -bound), bound).astype(kind)


def setup_inputs(seed: int = 0) -> dict:
    key_of = jax.random.split(jax.random.key(seed), 14)
    return {
        "positions": jnp.clip(60.0 * jax.random.uniform(key_of[0], (3, ATOMS), jnp.float32) ** block_scale(key_of[0], (3, ATOMS), ((1, 32),), -0.2, 0.2), 0.0, 60.0),
        "features": noise(key_of[1], (ATOMS, HID), 1.0, 6.0, ((0, 32),)),
        "nbr_index": set_ends(jax.random.randint(key_of[2], (ATOMS, NEIGH), 0, DOM_ATOMS + 2 * HALO), jax.random.fold_in(key_of[2], 1), 0, (DOM_ATOMS + 2 * HALO) - 1).astype(jnp.int32),
        "nbr_count": set_ends(jax.random.randint(key_of[3], (ATOMS,), NEIGH // 4, NEIGH + 1), jax.random.fold_in(key_of[3], 1), NEIGH // 4, NEIGH).astype(jnp.int32),
        "nbr_dist": jnp.clip(0.8 + 4.2 * jax.random.uniform(key_of[4], (ATOMS, NEIGH), jnp.float32) ** block_scale(key_of[4], (ATOMS, NEIGH), ((0, 32),), -0.2, 0.2), 0.8, 5.0),
        "halo_lists": set_ends(jax.random.randint(key_of[5], (DOMS, 2, HALO), 0, DOM_ATOMS), jax.random.fold_in(key_of[5], 1), 0, DOM_ATOMS - 1).astype(jnp.int32),
        "wave_vectors": draw_wave_vectors(jax.random.fold_in(key_of[13], 71), 0),
        "w_charge_first": noise(key_of[7], (HID, CHAN), HID ** -0.5, 0.5),
        "w_long_first": noise(key_of[8], (CHAN, HID), CHAN ** -0.5, 1.5, (), jnp.float32),
        "w_value": noise(key_of[9], (HID, HID), HID ** -0.5, 0.5),
        "w_filter": noise(key_of[10], (NRBF, HID), NRBF ** -0.5, 1.5, (), jnp.float32),
        "w_charge_second": noise(key_of[11], (HID, CHAN), HID ** -0.5, 0.5),
        "w_long_second": noise(key_of[12], (CHAN, HID), CHAN ** -0.5, 1.5, (), jnp.float32),
    }


HIGHEST_PRECISION = lax.Precision.HIGHEST
LONG_SCALE = 2.0

def wave_weight(wavevec):
    sq_norm = wavevec[0] * wavevec[0] + wavevec[1] * wavevec[1] + wavevec[2] * wavevec[2]
    return jnp.exp(-0.5 * sq_norm) / (sq_norm + 1.0)

def phase_tables(wavevec, coords):
    phase_angle = wavevec[0][:, None] * coords[0][None, :] + wavevec[1][:, None] * coords[1][None, :] + wavevec[2][:, None] * coords[2][None, :]
    return (jnp.cos(phase_angle), jnp.sin(phase_angle))

def partial_structure(wavevec, coords, charge):
    cos_table, sin_table = phase_tables(wavevec, coords)
    return (jnp.dot(cos_table, charge, precision=HIGHEST_PRECISION, preferred_element_type=jnp.float32), jnp.dot(sin_table, charge, precision=HIGHEST_PRECISION, preferred_element_type=jnp.float32))

def partial_project(wavevec, coords, charge, cos_part, sin_part):
    cos_table, sin_table = phase_tables(wavevec, coords)
    weight = wave_weight(wavevec)[:, None]
    cos_weighted = weight * cos_part
    sin_weighted = weight * sin_part
    contract_dims = (((0,), (0,)), ((), ()))
    potential = lax.dot_general(cos_table, cos_weighted, contract_dims, precision=HIGHEST_PRECISION, preferred_element_type=jnp.float32)
    potential = potential + lax.dot_general(sin_table, sin_weighted, contract_dims, precision=HIGHEST_PRECISION, preferred_element_type=jnp.float32)
    along_cos = jnp.dot(cos_weighted, charge.T, precision=HIGHEST_PRECISION, preferred_element_type=jnp.float32)
    along_sin = jnp.dot(sin_weighted, charge.T, precision=HIGHEST_PRECISION, preferred_element_type=jnp.float32)
    mixed = sin_table * along_cos - cos_table * along_sin
    force = jnp.dot(wavevec, mixed, precision=HIGHEST_PRECISION, preferred_element_type=jnp.float32)
    return (potential, force)

def long_range(hidden, w_charge, positions, wave_vectors):
    charge = jnp.dot(hidden, w_charge, preferred_element_type=jnp.float32)
    wave_block = min(256, KVEC)
    block_count = KVEC // wave_block
    wave_blocks = wave_vectors.reshape(3, block_count, wave_block).transpose(1, 0, 2)
    cos_part, sin_part = lax.map(lambda wavevec: partial_structure(wavevec, positions, charge), wave_blocks)
    inv_root = 1.0 / math.sqrt(ATOMS)
    cos_part = cos_part * inv_root
    sin_part = sin_part * inv_root

    def accumulate(running, member):
        pot_add, force_add = partial_project(member[0], positions, charge, member[1], member[2])
        return ((running[0] + pot_add, running[1] + force_add), None)
    start_state = (jnp.zeros((ATOMS, CHAN), jnp.float32), jnp.zeros((3, ATOMS), jnp.float32))
    (potential, force), _ = lax.scan(accumulate, start_state, (wave_blocks, cos_part, sin_part))
    prefactor = LONG_SCALE / math.sqrt(KVEC)
    return (potential * prefactor, force * prefactor)

def basis_of(distance, live_count):
    centers = 0.5 + 4.5 / (NRBF - 1) * jnp.arange(NRBF, dtype=jnp.int32).astype(jnp.float32)
    sharpness = ((NRBF - 1) / 4.5) ** 2
    envelope = 0.5 * (jnp.cos(math.pi * distance / 5.0) + 1.0)
    in_list = (jnp.arange(distance.shape[1], dtype=jnp.int32)[None, :] < live_count[:, None]).astype(jnp.float32)
    radial = jnp.exp(-sharpness * (distance[..., None] - centers) ** 2)
    return (radial * (envelope * in_list)[..., None]).astype(jnp.bfloat16)

def short_range(hidden, w_value, w_filter, nbr_index, nbr_count, nbr_dist, halo_lists):
    values = jnp.dot(hidden, w_value, preferred_element_type=jnp.float32).astype(jnp.bfloat16)
    by_domain = values.reshape(DOMS, DOM_ATOMS, HID)
    selected = jax.vmap(lambda rows_of, picks: rows_of[picks])(by_domain, halo_lists)
    from_below = jnp.roll(selected[:, 0], 1, axis=0)
    from_above = jnp.roll(selected[:, 1], -1, axis=0)
    value_table = jnp.concatenate([by_domain, from_below, from_above], axis=1)

    def one_domain(member):
        table_rows, index_rows, count_rows, dist_rows = member
        picked = table_rows[index_rows].astype(jnp.float32)
        basis = basis_of(dist_rows, count_rows).astype(jnp.float32)
        contracted = jnp.einsum('ajr,ajf->arf', basis, picked, precision=HIGHEST_PRECISION)
        return jnp.einsum('arf,rf->af', contracted, w_filter, precision=HIGHEST_PRECISION)
    message = lax.map(one_domain, (value_table, nbr_index.reshape(DOMS, DOM_ATOMS, NEIGH), nbr_count.reshape(DOMS, DOM_ATOMS), nbr_dist.reshape(DOMS, DOM_ATOMS, NEIGH))).reshape(ATOMS, HID)
    return (hidden.astype(jnp.float32) + jax.nn.silu(message)).astype(jnp.bfloat16)

def reference(positions, features, nbr_index, nbr_count, nbr_dist, halo_lists, wave_vectors, w_charge_first, w_long_first, w_value, w_filter, w_charge_second, w_long_second):
    pot_first, force_first = long_range(features, w_charge_first, positions, wave_vectors)
    lifted = jnp.dot(pot_first, w_long_first, precision=HIGHEST_PRECISION, preferred_element_type=jnp.float32)
    hidden_first = (features.astype(jnp.float32) + jax.nn.silu(lifted)).astype(jnp.bfloat16)
    hidden_second = short_range(hidden_first, w_value, w_filter, nbr_index, nbr_count, nbr_dist, halo_lists)
    pot_second, force_second = long_range(hidden_second, w_charge_second, positions, wave_vectors)
    lifted = jnp.dot(pot_second, w_long_second, precision=HIGHEST_PRECISION, preferred_element_type=jnp.float32)
    features_out = (hidden_second.astype(jnp.float32) + jax.nn.silu(lifted)).astype(jnp.bfloat16)
    return (features_out, force_first + force_second)
```

```python
import functools
import math

import jax
import jax.numpy as jnp
from jax import lax
from jax.experimental import pallas as pl
from jax.experimental.pallas import tpu as pltpu
from jax.sharding import PartitionSpec as P

MESH = pl.DeviceIdType.MESH
LONG_SCALE = 2.0
LANES = 128
F32 = jnp.float32
BF16 = jnp.bfloat16
SIN_TURN = (
    6.283185005187988,
    -41.341590881347656,
    81.59994506835938,
    -76.61447143554688,
    41.3428840637207,
    -12.471243858337402,
)
COS_TURN = (
    0.9999992251396179,
    -19.738981246948242,
    64.92865753173828,
    -85.27162170410156,
    58.79049301147461,
    -21.07110595703125,
)


def contract(a, b, dim_a, dim_b):
    return lax.dot_general(
        a, b, (((dim_a,), (dim_b,)), ((), ())), preferred_element_type=F32
    )


def halves(x):
    high = x.astype(BF16)
    return high, (x - high.astype(F32)).astype(BF16)


def horner(coefs, x):
    value = jnp.full_like(x, coefs[-1])
    for coef in coefs[-2::-1]:
        value = value * x + coef
    return value


def silu(x):
    return x / (1.0 + jnp.exp(-x))


def kernel(
    doms,
    kvs,
    total_atoms,
    pos_ref,
    feat_ref,
    idx_ref,
    cnt_ref,
    dist_ref,
    halo_ref,
    wave_ref,
    wc1_ref,
    wl1_ref,
    wv_ref,
    wf_ref,
    wc2_ref,
    wl2_ref,
    out_ref,
    force_ref,
    posb,
    cos_tab,
    sin_tab,
    send,
    recv,
    result,
    vals,
    halo_out,
    halo_in,
    table,
    basis,
    filt,
    idx_t,
    message,
    red_send_sem,
    red_recv_sem,
    bc_send_sem,
    bc_recv_sem,
    val_send_sem,
    val_recv_sem,
    halo_send_sem,
    halo_recv_sem,
):
    n = doms * kvs
    atoms, hid = feat_ref.shape
    waves = wave_ref.shape[1]
    chan = wc1_ref.shape[1]
    slots = idx_ref.shape[1]
    radial = wf_ref.shape[0]
    halo = halo_ref.shape[1]
    dom_atoms = kvs * atoms
    wave_tiles = waves // LANES
    chunks = 2 * wave_tiles
    my_dom = lax.axis_index("dom")
    my_kv = lax.axis_index("kv")
    me = my_dom * kvs + my_kv

    def device(i):
        return (lax.div(i, kvs), lax.rem(i, kvs))

    barrier = pltpu.get_barrier_semaphore()

    def greet(step, _):
        pl.semaphore_signal(
            barrier, inc=1, device_id=device(lax.rem(me + step, n)), device_id_type=MESH
        )
        return 0

    lax.fori_loop(1, n, greet, 0)

    pos = pos_ref[...] * (1.0 / (2.0 * math.pi))
    pos_cols = jnp.concatenate([pos, jnp.zeros((5, atoms), F32)], axis=0).T
    for d in range(3):
        posb[d] = jnp.broadcast_to(pos_cols[:, d : d + 1], (atoms, LANES))

    def table_tile(tile, _):
        cols = pl.ds(pl.multiple_of(tile * LANES, LANES), LANES)
        turns = (
            posb[0] * wave_ref[0:1, cols]
            + posb[1] * wave_ref[1:2, cols]
            + posb[2] * wave_ref[2:3, cols]
        )
        turns = turns - jnp.round(turns)
        square = turns * turns
        cos_tab[:, cols] = horner(COS_TURN, square).astype(BF16)
        sin_tab[:, cols] = (horner(SIN_TURN, square) * turns).astype(BF16)
        return 0

    lax.fori_loop(0, wave_tiles, table_tile, 0)

    kx, ky, kz = wave_ref[0:1, :], wave_ref[1:2, :], wave_ref[2:3, :]
    sq_norm = kx * kx + ky * ky + kz * kz
    weight = jnp.exp(-0.5 * sq_norm) / (sq_norm + 1.0)
    weight = weight * (LONG_SCALE / math.sqrt(waves) / math.sqrt(total_atoms))

    def start_structure(block, charge):
        high, low = halves(charge)
        both = jnp.concatenate([high, low], axis=0)
        for half, tab in enumerate((cos_tab, sin_tab)):
            part = contract(both, tab[...], 1, 0)
            part = (part[:chan] + part[chan:]).astype(BF16)
            for tile in range(wave_tiles):
                send[block, half * wave_tiles + tile] = part[:, tile * LANES : (tile + 1) * LANES]

    def send_partials(block):
        def put(step, _):
            peer = lax.rem(me + step, n)

            def go():
                pltpu.make_async_remote_copy(
                    src_ref=send.at[block, peer],
                    dst_ref=recv.at[block, step - 1],
                    send_sem=red_send_sem.at[block],
                    recv_sem=red_recv_sem.at[block],
                    device_id=device(peer),
                    device_id_type=MESH,
                ).start()

            if n > chunks:
                pl.when(peer < chunks)(go)
            else:
                go()
            return 0

        lax.fori_loop(1, n, put, 0)

    def wait_bytes(ref, sem):
        pltpu.make_async_copy(ref, ref, sem).wait()

    def reduce_and_share(block):
        def own():
            wait_bytes(recv.at[block], red_recv_sem.at[block])
            total = send[block, me].astype(F32)
            for step in range(n - 1):
                total = total + recv[block, step].astype(F32)
            result[block, me] = total.astype(BF16)

            def put(step, _):
                pltpu.make_async_remote_copy(
                    src_ref=result.at[block, me],
                    dst_ref=result.at[block, me],
                    send_sem=bc_send_sem.at[block],
                    recv_sem=bc_recv_sem.at[block],
                    device_id=device(lax.rem(me + step, n)),
                    device_id_type=MESH,
                ).start()
                return 0

            lax.fori_loop(1, n, put, 0)
            wait_bytes(result.at[block, pl.ds(0, chunks - 1)], bc_recv_sem.at[block])

        if n > chunks:
            pl.when(me < chunks)(own)

            @pl.when(me >= chunks)
            def _():
                wait_bytes(result.at[block], bc_recv_sem.at[block])
        else:
            own()

    def finish_sends(block):
        def own():
            wait_bytes(send.at[block, pl.ds(0, chunks - 1)], red_send_sem.at[block])
            wait_bytes(recv.at[block], bc_send_sem.at[block])

        if n > chunks:
            pl.when(me < chunks)(own)

            @pl.when(me >= chunks)
            def _():
                wait_bytes(send.at[block], red_send_sem.at[block])
        else:
            own()

    def project(block, charge):
        full = [
            jnp.concatenate(
                [result[block, half * wave_tiles + tile] for tile in range(wave_tiles)], axis=1
            ).astype(F32)
            * weight
            for half in (0, 1)
        ]
        cos_w, sin_w = full
        on_cos = jnp.concatenate([cos_w, -kx * sin_w, -ky * sin_w, -kz * sin_w], axis=0)
        on_sin = jnp.concatenate([sin_w, kx * cos_w, ky * cos_w, kz * cos_w], axis=0)
        out = contract(jnp.concatenate(halves(on_cos), axis=0), cos_tab[...], 1, 1)
        out = out + contract(jnp.concatenate(halves(on_sin), axis=0), sin_tab[...], 1, 1)
        rows = 4 * chan
        out = out[:rows] + out[rows:]
        force = [
            jnp.sum(charge * out[chan * (d + 1) : chan * (d + 2)], axis=0, keepdims=True)
            for d in range(3)
        ]
        return out[:chan], jnp.concatenate(force, axis=0)

    def lift(pot, wl_ref):
        high, low = halves(pot)
        w_high, w_low = halves(wl_ref[...])
        return contract(
            jnp.concatenate([high, low, high], axis=0),
            jnp.concatenate([w_high, w_high, w_low], axis=0),
            0,
            0,
        )

    features = feat_ref[...]
    charge = contract(wc1_ref[...], features, 0, 1)
    start_structure(0, charge)
    pl.semaphore_wait(barrier, n - 1)
    send_partials(0)

    idx_t[...] = jnp.concatenate(
        [idx_ref[...], jnp.zeros((atoms, LANES - slots), jnp.int32)], axis=1
    ).T[:slots]
    dist_t = jnp.concatenate([dist_ref[...], jnp.ones((atoms, LANES - slots), F32)], axis=1).T[
        :slots
    ]
    slot_row = lax.broadcasted_iota(jnp.int32, (slots, atoms), 0)
    envelope = 0.5 * (jnp.cos(math.pi * dist_t / 5.0) + 1.0)
    envelope = jnp.where(slot_row < cnt_ref[...], envelope, 0.0)
    centers = 0.5 + 4.5 / (radial - 1) * lax.broadcasted_iota(jnp.int32, (radial, atoms), 0).astype(
        F32
    )
    sharpness = ((radial - 1) / 4.5) ** 2
    for s in range(slots):
        away = dist_t[s : s + 1] - centers
        basis[s] = (jnp.exp(-sharpness * (away * away)) * envelope[s : s + 1]).astype(BF16)
    filt[...] = wf_ref[...].T.astype(BF16)

    reduce_and_share(0)
    pot, force = project(0, charge)
    hidden = (features.astype(F32) + silu(lift(pot, wl1_ref))).astype(BF16)

    values = contract(wv_ref[...], hidden, 0, 1).astype(BF16)
    vals[my_kv] = values

    def put_values(step, _):
        peer = lax.rem(my_kv + step, kvs)
        pltpu.make_async_remote_copy(
            src_ref=vals.at[my_kv],
            dst_ref=vals.at[my_kv],
            send_sem=val_send_sem,
            recv_sem=val_recv_sem,
            device_id=(my_dom, peer),
            device_id_type=MESH,
        ).start()
        return 0

    lax.fori_loop(1, kvs, put_values, 0)
    wait_bytes(vals.at[pl.ds(0, kvs - 1)], val_recv_sem)
    for q in range(kvs):
        table[0:hid, q * atoms : (q + 1) * atoms] = vals[q]
    own_rows = lax.broadcasted_iota(jnp.int32, (dom_atoms, halo), 0)
    copies = []
    for side, turn in ((0, 1), (1, doms - 1)):
        picks = jnp.where(own_rows == halo_ref[side : side + 1, :], 1.0, 0.0).astype(BF16)
        halo_out[side] = contract(table[0:hid, :], picks, 1, 0).astype(BF16)
        copy = pltpu.make_async_remote_copy(
            src_ref=halo_out.at[side],
            dst_ref=halo_in.at[side],
            send_sem=halo_send_sem.at[side],
            recv_sem=halo_recv_sem.at[side],
            device_id=(lax.rem(my_dom + turn, doms), my_kv),
            device_id_type=MESH,
        )
        copy.start()
        copies.append(copy)
    for side, copy in enumerate(copies):
        copy.wait()
        table[hid:, side * halo : (side + 1) * halo] = halo_in[side]

    message[...] = jnp.zeros_like(message)
    rows_of = lax.broadcasted_iota(jnp.int32, (dom_atoms, atoms), 0)

    def one_slot(s, _):
        index = idx_t[pl.ds(s, 1), :]
        outside = index >= dom_atoms
        index = jnp.where(outside, index - dom_atoms, index)
        picks = jnp.where(rows_of == index, 1.0, 0.0).astype(BF16)
        picked = contract(table[...], picks, 1, 0)
        scale = contract(filt[...], basis[s], 1, 0)
        message[...] += scale * jnp.where(outside, picked[hid:], picked[:hid])
        return 0

    lax.fori_loop(0, slots, one_slot, 0, unroll=2)
    hidden = (hidden.astype(F32) + silu(message[...]).T).astype(BF16)

    charge = contract(wc2_ref[...], hidden, 0, 1)
    start_structure(1, charge)
    send_partials(1)
    reduce_and_share(1)
    pot, force_second = project(1, charge)
    out_ref[...] = (hidden.astype(F32) + silu(lift(pot, wl2_ref))).astype(BF16)
    force_ref[...] = force + force_second

    wait_bytes(vals.at[pl.ds(0, kvs - 1)], val_send_sem)
    finish_sends(0)
    finish_sends(1)


def local(doms, kvs, *args):
    (positions, features, nbr_index, nbr_count, nbr_dist, halo_lists, wave_vectors) = args[:7]
    weights = args[7:]
    n = doms * kvs
    atoms, hid = features.shape
    waves = wave_vectors.shape[1]
    slots = nbr_index.shape[1]
    radial = weights[3].shape[0]
    halo = halo_lists.shape[2]
    chan = weights[0].shape[1]
    chunks = 2 * waves // LANES
    dom_atoms = kvs * atoms
    sem = pltpu.SemaphoreType.DMA
    vmem = pl.BlockSpec(memory_space=pltpu.VMEM)
    return tuple(
        pl.pallas_call(
            functools.partial(kernel, doms, kvs, n * atoms),
            out_shape=(
                jax.ShapeDtypeStruct((atoms, hid), BF16),
                jax.ShapeDtypeStruct((3, atoms), F32),
            ),
            in_specs=[vmem] * 13,
            out_specs=(vmem, vmem),
            scratch_shapes=[
                pltpu.VMEM((3, atoms, LANES), F32),
                pltpu.VMEM((atoms, waves), BF16),
                pltpu.VMEM((atoms, waves), BF16),
                pltpu.VMEM((2, chunks, chan, LANES), BF16),
                pltpu.VMEM((2, n - 1, chan, LANES), BF16),
                pltpu.VMEM((2, chunks, chan, LANES), BF16),
                pltpu.VMEM((kvs, hid, atoms), BF16),
                pltpu.VMEM((2, hid, halo), BF16),
                pltpu.VMEM((2, hid, halo), BF16),
                pltpu.VMEM((2 * hid, dom_atoms), BF16),
                pltpu.VMEM((slots, radial, atoms), BF16),
                pltpu.VMEM((hid, radial), BF16),
                pltpu.VMEM((slots, atoms), jnp.int32),
                pltpu.VMEM((hid, atoms), F32),
                sem((2,)),
                sem((2,)),
                sem((2,)),
                sem((2,)),
                sem,
                sem,
                sem((2,)),
                sem((2,)),
            ],
            compiler_params=pltpu.CompilerParams(
                collective_id=0, has_side_effects=True, vmem_limit_bytes=48 * 1024 * 1024
            ),
        )(
            positions,
            features,
            nbr_index,
            nbr_count.reshape(1, atoms),
            nbr_dist,
            halo_lists.reshape(2, halo),
            wave_vectors,
            *weights,
        )
    )


def solution(mesh):
    return jax.shard_map(
        functools.partial(local, mesh.shape["dom"], mesh.shape["kv"]),
        mesh=mesh,
        in_specs=(
            P(None, ("dom", "kv")),
            P(("dom", "kv"), None),
            P(("dom", "kv"), None),
            P(("dom", "kv")),
            P(("dom", "kv"), None),
            P("dom", None, None),
            P(),
            P(),
            P(),
            P(),
            P(),
            P(),
            P(),
        ),
        out_specs=(P(("dom", "kv"), None), P(None, ("dom", "kv"))),
        check_vma=False,
    )
```

```python
import functools
import math

import jax
import jax.numpy as jnp
from jax import lax
from jax.experimental import pallas as pl
from jax.experimental.pallas import tpu as pltpu
from jax.sharding import PartitionSpec as P

MESH = pl.DeviceIdType.MESH
LONG_SCALE = 2.0
LANES = 128
F32 = jnp.float32
BF16 = jnp.bfloat16
SIN_TURN = (
    6.283185005187988,
    -41.341590881347656,
    81.59994506835938,
    -76.61447143554688,
    41.3428840637207,
    -12.471243858337402,
)
COS_TURN = (
    0.9999992251396179,
    -19.738981246948242,
    64.92865753173828,
    -85.27162170410156,
    58.79049301147461,
    -21.07110595703125,
)


def contract(a, b, dim_a, dim_b):
    return lax.dot_general(
        a, b, (((dim_a,), (dim_b,)), ((), ())), preferred_element_type=F32
    )


def halves(x):
    high = x.astype(BF16)
    return high, (x - high.astype(F32)).astype(BF16)


def horner(coefs, x):
    value = jnp.full_like(x, coefs[-1])
    for coef in coefs[-2::-1]:
        value = value * x + coef
    return value


def silu(x):
    return x / (1.0 + jnp.exp(-x))


def kernel(
    doms,
    kvs,
    total_atoms,
    pos_ref,
    feat_ref,
    idx_ref,
    cnt_ref,
    dist_ref,
    halo_ref,
    wave_ref,
    wc1_ref,
    wl1_ref,
    wv_ref,
    wf_ref,
    wc2_ref,
    wl2_ref,
    out_ref,
    force_ref,
    posb,
    cos_tab,
    sin_tab,
    send,
    recv,
    result,
    near_pos,
    near_feat,
    near_hidden,
    halo_out,
    table,
    basis,
    scale,
    low_rows,
    high_row,
    message,
    red_send_sem,
    red_recv_sem,
    bc_send_sem,
    bc_recv_sem,
    pos_send_sem,
    pos_recv_sem,
    feat_send_sem,
    feat_recv_sem,
    halo_send_sem,
    halo_recv_sem,
):
    n = doms * kvs
    atoms, hid = feat_ref.shape
    waves = wave_ref.shape[1]
    chan = wc1_ref.shape[0]
    slots = idx_ref.shape[0]
    radial = wf_ref.shape[0]
    halo = halo_ref.shape[1]
    halo_ways = halo // atoms
    wave_tiles = waves // LANES
    chunks = 2 * wave_tiles
    my_dom = lax.axis_index("dom")
    my_kv = lax.axis_index("kv")
    me = my_dom * kvs + my_kv

    def device(i):
        return (lax.div(i, kvs), lax.rem(i, kvs))

    barrier = pltpu.get_barrier_semaphore()

    def greet(step, _):
        pl.semaphore_signal(
            barrier, inc=1, device_id=device(lax.rem(me + step, n)), device_id_type=MESH
        )
        return 0

    lax.fori_loop(1, n, greet, 0)

    def fill_tables(slot):
        pos = near_pos[slot] * (1.0 / (2.0 * math.pi))
        pos_cols = pos.T
        for d in range(3):
            posb[d] = jnp.broadcast_to(pos_cols[:, d : d + 1], (atoms, LANES))

        def table_tile(tile, _):
            cols = pl.ds(pl.multiple_of(tile * LANES, LANES), LANES)
            turns = (
                posb[0] * wave_ref[0:1, cols]
                + posb[1] * wave_ref[1:2, cols]
                + posb[2] * wave_ref[2:3, cols]
            )
            turns = turns - jnp.round(turns)
            square = turns * turns
            cos_tab[slot, :, cols] = horner(COS_TURN, square).astype(BF16)
            sin_tab[slot, :, cols] = (horner(SIN_TURN, square) * turns).astype(BF16)
            return 0

        lax.fori_loop(0, wave_tiles, table_tile, 0)

    near_pos[0] = jnp.concatenate([pos_ref[...], jnp.zeros((5, atoms), F32)], axis=0)
    near_feat[0] = feat_ref[...]
    fill_tables(0)

    kx, ky, kz = wave_ref[0:1, :], wave_ref[1:2, :], wave_ref[2:3, :]
    sq_norm = kx * kx + ky * ky + kz * kz
    weight = jnp.exp(-0.5 * sq_norm) / (sq_norm + 1.0)
    weight = weight * (LONG_SCALE / math.sqrt(waves) / math.sqrt(total_atoms))

    def start_structure(block, charge):
        high, low = halves(charge)
        both = jnp.concatenate([high, low], axis=0)
        for half, tab in enumerate((cos_tab, sin_tab)):
            part = contract(both, tab[0], 1, 0)
            part = (part[:chan] + part[chan:]).astype(BF16)
            for tile in range(wave_tiles):
                send[block, half * wave_tiles + tile] = part[:, tile * LANES : (tile + 1) * LANES]

    def send_partials(block):
        def put(step, _):
            peer = lax.rem(me + step, n)

            def go():
                pltpu.make_async_remote_copy(
                    src_ref=send.at[block, peer],
                    dst_ref=recv.at[block, step - 1],
                    send_sem=red_send_sem.at[block],
                    recv_sem=red_recv_sem.at[block],
                    device_id=device(peer),
                    device_id_type=MESH,
                ).start()

            if n > chunks:
                pl.when(peer < chunks)(go)
            else:
                go()
            return 0

        lax.fori_loop(1, n, put, 0)

    def wait_bytes(ref, sem):
        pltpu.make_async_copy(ref, ref, sem).wait()

    def reduce_and_share(block):
        def own():
            wait_bytes(recv.at[block], red_recv_sem.at[block])
            total = send[block, me].astype(F32)
            for step in range(n - 1):
                total = total + recv[block, step].astype(F32)
            result[block, me] = total.astype(BF16)

            def put(step, _):
                pltpu.make_async_remote_copy(
                    src_ref=result.at[block, me],
                    dst_ref=result.at[block, me],
                    send_sem=bc_send_sem.at[block],
                    recv_sem=bc_recv_sem.at[block],
                    device_id=device(lax.rem(me + step, n)),
                    device_id_type=MESH,
                ).start()
                return 0

            lax.fori_loop(1, n, put, 0)
            wait_bytes(result.at[block, pl.ds(0, chunks - 1)], bc_recv_sem.at[block])

        if n > chunks:
            pl.when(me < chunks)(own)

            @pl.when(me >= chunks)
            def _():
                wait_bytes(result.at[block], bc_recv_sem.at[block])
        else:
            own()

    def finish_sends(block):
        def own():
            wait_bytes(send.at[block, pl.ds(0, chunks - 1)], red_send_sem.at[block])
            wait_bytes(recv.at[block], bc_send_sem.at[block])

        if n > chunks:
            pl.when(me < chunks)(own)

            @pl.when(me >= chunks)
            def _():
                wait_bytes(send.at[block], red_send_sem.at[block])
        else:
            own()

    def weighted(block):
        return [
            jnp.concatenate(
                [result[block, half * wave_tiles + tile] for tile in range(wave_tiles)], axis=1
            ).astype(F32)
            * weight
            for half in (0, 1)
        ]

    def project(cos_w, sin_w, charge):
        on_cos = jnp.concatenate([cos_w, -kx * sin_w, -ky * sin_w, -kz * sin_w], axis=0)
        on_sin = jnp.concatenate([sin_w, kx * cos_w, ky * cos_w, kz * cos_w], axis=0)
        out = contract(jnp.concatenate(halves(on_cos), axis=0), cos_tab[0], 1, 1)
        out = out + contract(jnp.concatenate(halves(on_sin), axis=0), sin_tab[0], 1, 1)
        rows = 4 * chan
        out = out[:rows] + out[rows:]
        force = [
            jnp.sum(charge * out[chan * (d + 1) : chan * (d + 2)], axis=0, keepdims=True)
            for d in range(3)
        ]
        return out[:chan], jnp.concatenate(force, axis=0)

    def potential(cos_w, sin_w, slot):
        out = contract(jnp.concatenate(halves(cos_w), axis=0), cos_tab[slot], 1, 1)
        out = out + contract(jnp.concatenate(halves(sin_w), axis=0), sin_tab[slot], 1, 1)
        return out[:chan] + out[chan:]

    def lift(pot, wl_ref):
        high, low = halves(pot)
        w_high, w_low = halves(wl_ref[...])
        return contract(
            jnp.concatenate([high, low, high], axis=0),
            jnp.concatenate([w_high, w_high, w_low], axis=0),
            0,
            0,
        )

    features = feat_ref[...]
    charge = contract(wc1_ref[...], features, 1, 1)
    start_structure(0, charge)
    pl.semaphore_wait(barrier, n - 1)
    send_partials(0)

    def put_near(step, _):
        peer = device(my_dom * kvs + lax.rem(my_kv + step, kvs))
        for ref, send_sem, recv_sem in (
            (near_pos, pos_send_sem, pos_recv_sem),
            (near_feat, feat_send_sem, feat_recv_sem),
        ):
            pltpu.make_async_remote_copy(
                src_ref=ref.at[0],
                dst_ref=ref.at[kvs - step],
                send_sem=send_sem,
                recv_sem=recv_sem,
                device_id=peer,
                device_id_type=MESH,
            ).start()
        return 0

    lax.fori_loop(1, kvs, put_near, 0)

    dist_t = dist_ref[...]
    slot_row = lax.broadcasted_iota(jnp.int32, (slots, atoms), 0)
    envelope = 0.5 * (jnp.cos(math.pi * dist_t / 5.0) + 1.0)
    envelope = jnp.where(slot_row < cnt_ref[...], envelope, 0.0)
    centers = 0.5 + 4.5 / (radial - 1) * lax.broadcasted_iota(jnp.int32, (radial, atoms), 0).astype(
        F32
    )
    sharpness = ((radial - 1) / 4.5) ** 2
    group = 256 // radial
    for s in range(slots):
        away = dist_t[s : s + 1] - centers
        values = jnp.exp(-sharpness * (away * away)) * envelope[s : s + 1]
        basis[s // group, (s % group) * radial : (s % group + 1) * radial] = values.astype(BF16)
    column = lax.broadcasted_iota(jnp.int32, (radial, 256), 1)
    row = lax.broadcasted_iota(jnp.int32, (radial, 256), 0)
    repeat = jnp.where(lax.rem(column, radial) == row, 1.0, 0.0).astype(BF16)
    wide = contract(wf_ref[...].astype(BF16), repeat, 0, 0)
    member = lax.div(lax.broadcasted_iota(jnp.int32, (hid, 256), 1), radial)
    filt = jnp.concatenate(
        [jnp.where(member == s, wide, 0.0).astype(BF16) for s in range(group)], axis=0
    )

    def one_group(g, _):
        scale[pl.ds(g * group, group)] = contract(filt, basis[g], 1, 0).reshape(group, hid, atoms)
        return 0

    lax.fori_loop(0, slots // group, one_group, 0)
    index = idx_ref[...]
    high_row[...] = lax.div(index, atoms)
    low = lax.rem(index, atoms).astype(F32)
    for s in range(slots):
        low_rows[s] = jnp.broadcast_to(low[s : s + 1], (16, atoms)).astype(BF16)

    wait_bytes(near_pos.at[pl.ds(1, kvs - 1)], pos_recv_sem)
    wait_bytes(near_feat.at[pl.ds(1, kvs - 1)], feat_recv_sem)

    def near_tables(slot, _):
        fill_tables(slot)
        return 0

    lax.fori_loop(1, kvs, near_tables, 0)

    reduce_and_share(0)
    cos_w, sin_w = weighted(0)

    def domain_values(slot, _):
        pot = potential(cos_w, sin_w, slot)
        hidden = (near_feat[slot].astype(F32) + silu(lift(pot, wl1_ref))).astype(BF16)
        near_hidden[slot] = hidden
        values = contract(wv_ref[...], hidden, 0, 1).astype(BF16)
        table[lax.rem(my_kv + slot, kvs)] = values
        return 0

    lax.fori_loop(0, kvs, domain_values, 0)
    own_rows = lax.broadcasted_iota(jnp.int32, (atoms, atoms), 0)
    copies = []
    for side, turn in ((0, 1), (1, doms - 1)):
        for way in range(halo_ways):
            wanted = halo_ref[side : side + 1, way * atoms : (way + 1) * atoms]
            total = jnp.zeros((hid, atoms), F32)
            for q in range(kvs):
                picks = jnp.where(own_rows + q * atoms == wanted, 1.0, 0.0).astype(BF16)
                total = total + contract(table[q], picks, 1, 0)
            halo_out[side, way] = total.astype(BF16)
        copy = pltpu.make_async_remote_copy(
            src_ref=halo_out.at[side],
            dst_ref=table.at[pl.ds(kvs + side * halo_ways, halo_ways)],
            send_sem=halo_send_sem.at[side],
            recv_sem=halo_recv_sem.at[side],
            device_id=device(lax.rem(my_dom + turn, doms) * kvs + my_kv),
            device_id_type=MESH,
        )
        copy.start()
        copies.append(copy)
    pot, force = project(cos_w, sin_w, charge)
    for copy in copies:
        copy.wait()

    ways = kvs + 2 * halo_ways
    row_ids = lax.broadcasted_iota(jnp.int32, (atoms, atoms), 0).astype(F32).astype(BF16)
    row_ids = row_ids.reshape(atoms // 16, 16, atoms)
    one, zero = jnp.ones((), BF16), jnp.zeros((), BF16)
    message[...] = jnp.zeros_like(message)
    together = 4

    def some_slots(step, _):
        total = message[...]
        for s in range(together):
            s = step * together + s
            picks = jnp.where(row_ids == low_rows[s][None], one, zero).reshape(atoms, atoms)
            picked = contract(table[...].reshape(ways * hid, atoms), picks, 1, 0)
            high = high_row[pl.ds(s, 1), :]
            value = picked[:hid]
            for way in range(1, ways):
                value = jnp.where(high == way, picked[way * hid : (way + 1) * hid], value)
            total = total + scale[s] * value
        message[...] = total
        return 0

    lax.fori_loop(0, slots // together, some_slots, 0)
    hidden = (near_hidden[0].astype(F32) + silu(message[...]).T).astype(BF16)

    charge = contract(wc2_ref[...], hidden, 1, 1)
    start_structure(1, charge)
    send_partials(1)
    reduce_and_share(1)
    pot, force_second = project(*weighted(1), charge)
    out_ref[...] = (hidden.astype(F32) + silu(lift(pot, wl2_ref))).astype(BF16)
    force_ref[...] = force + force_second

    wait_bytes(near_pos.at[pl.ds(1, kvs - 1)], pos_send_sem)
    wait_bytes(near_feat.at[pl.ds(1, kvs - 1)], feat_send_sem)
    finish_sends(0)
    finish_sends(1)


def local(doms, kvs, *args):
    (positions, features, nbr_index, nbr_count, nbr_dist, halo_lists, wave_vectors) = args[:7]
    weights = args[7:]
    n = doms * kvs
    atoms, hid = features.shape
    waves = wave_vectors.shape[1]
    slots = nbr_index.shape[1]
    radial = weights[3].shape[0]
    halo = halo_lists.shape[2]
    chan = weights[0].shape[1]
    ways = kvs + 2 * (halo // atoms)
    chunks = 2 * waves // LANES
    sem = pltpu.SemaphoreType.DMA
    vmem = pl.BlockSpec(memory_space=pltpu.VMEM)
    return tuple(
        pl.pallas_call(
            functools.partial(kernel, doms, kvs, n * atoms),
            out_shape=(
                jax.ShapeDtypeStruct((atoms, hid), BF16),
                jax.ShapeDtypeStruct((3, atoms), F32),
            ),
            in_specs=[vmem] * 13,
            out_specs=(vmem, vmem),
            scratch_shapes=[
                pltpu.VMEM((3, atoms, LANES), F32),
                pltpu.VMEM((kvs, atoms, waves), BF16),
                pltpu.VMEM((kvs, atoms, waves), BF16),
                pltpu.VMEM((2, chunks, chan, LANES), BF16),
                pltpu.VMEM((2, n - 1, chan, LANES), BF16),
                pltpu.VMEM((2, chunks, chan, LANES), BF16),
                pltpu.VMEM((kvs, 8, atoms), F32),
                pltpu.VMEM((kvs, atoms, hid), BF16),
                pltpu.VMEM((kvs, atoms, hid), BF16),
                pltpu.VMEM((2, halo // atoms, hid, atoms), BF16),
                pltpu.VMEM((ways, hid, atoms), BF16),
                pltpu.VMEM((slots * radial // 256, 256, atoms), BF16),
                pltpu.VMEM((slots, hid, atoms), F32),
                pltpu.VMEM((slots, 16, atoms), BF16),
                pltpu.VMEM((slots, atoms), jnp.int32),
                pltpu.VMEM((hid, atoms), F32),
                sem((2,)),
                sem((2,)),
                sem((2,)),
                sem((2,)),
                sem,
                sem,
                sem,
                sem,
                sem((2,)),
                sem((2,)),
            ],
            compiler_params=pltpu.CompilerParams(
                collective_id=0, has_side_effects=True, vmem_limit_bytes=48 * 1024 * 1024
            ),
        )(
            positions,
            features,
            nbr_index.T,
            nbr_count.reshape(1, atoms),
            nbr_dist.T,
            halo_lists.reshape(2, halo),
            wave_vectors,
            weights[0].T,
            weights[1],
            weights[2],
            weights[3],
            weights[4].T,
            weights[5],
        )
    )


def solution(mesh):
    return jax.shard_map(
        functools.partial(local, mesh.shape["dom"], mesh.shape["kv"]),
        mesh=mesh,
        in_specs=(
            P(None, ("dom", "kv")),
            P(("dom", "kv"), None),
            P(("dom", "kv"), None),
            P(("dom", "kv")),
            P(("dom", "kv"), None),
            P("dom", None, None),
            P(),
            P(),
            P(),
            P(),
            P(),
            P(),
            P(),
        ),
        out_specs=(P(("dom", "kv"), None), P(None, ("dom", "kv"))),
        check_vma=False,
    )
```

```python
import functools
import math

import jax
import jax.numpy as jnp
from jax import lax
from jax.experimental import pallas as pl
from jax.experimental.pallas import tpu as pltpu
from jax.sharding import PartitionSpec as P

MESH = pl.DeviceIdType.MESH
LONG_SCALE = 2.0
LANES = 128
F32 = jnp.float32
BF16 = jnp.bfloat16
SIN_TURN = (
    6.283185005187988,
    -41.341590881347656,
    81.59994506835938,
    -76.61447143554688,
    41.3428840637207,
    -12.471243858337402,
)
COS_TURN = (
    0.9999992251396179,
    -19.738981246948242,
    64.92865753173828,
    -85.27162170410156,
    58.79049301147461,
    -21.07110595703125,
)


def contract(a, b, dim_a, dim_b):
    return lax.dot_general(
        a, b, (((dim_a,), (dim_b,)), ((), ())), preferred_element_type=F32
    )


def halves(x):
    high = x.astype(BF16)
    return high, (x - high.astype(F32)).astype(BF16)


def horner(coefs, x):
    value = jnp.full_like(x, coefs[-1])
    for coef in coefs[-2::-1]:
        value = value * x + coef
    return value


def silu(x):
    return x / (1.0 + jnp.exp(-x))


def kernel(doms, kvs, total_atoms, *refs):
    hbm_refs, refs = refs[:13], refs[13:]
    body(doms, kvs, total_atoms, hbm_refs, *refs)


def body(
    doms,
    kvs,
    total_atoms,
    hbm_refs,
    out_ref,
    force_ref,
    posb,
    cos_tab,
    sin_tab,
    send,
    recv,
    result,
    near_pos,
    near_feat,
    near_hidden,
    halo_out,
    table,
    basis,
    scale,
    low_rows,
    high_row,
    message,
    red_send_sem,
    red_recv_sem,
    bc_send_sem,
    bc_recv_sem,
    pos_send_sem,
    pos_recv_sem,
    feat_send_sem,
    feat_recv_sem,
    halo_send_sem,
    halo_recv_sem,
    in_sem,
    *in_refs,
):
    (
        pos_ref,
        feat_ref,
        idx_ref,
        cnt_ref,
        dist_ref,
        halo_ref,
        wave_ref,
        wc1_ref,
        wl1_ref,
        wv_ref,
        wf_ref,
        wc2_ref,
        wl2_ref,
    ) = in_refs
    fetches = [
        pltpu.make_async_copy(source, target, in_sem.at[i])
        for i, (source, target) in enumerate(zip(hbm_refs, in_refs))
    ]
    first_needed = (0, 1, 6, 7)
    for i in first_needed:
        fetches[i].start()
    n = doms * kvs
    atoms, hid = feat_ref.shape
    waves = wave_ref.shape[1]
    chan = wc1_ref.shape[0]
    slots = idx_ref.shape[0]
    radial = wf_ref.shape[0]
    halo = halo_ref.shape[1]
    halo_ways = halo // atoms
    wave_tiles = waves // LANES
    chunks = 2 * wave_tiles
    my_dom = lax.axis_index("dom")
    my_kv = lax.axis_index("kv")
    me = my_dom * kvs + my_kv

    def device(i):
        return (lax.div(i, kvs), lax.rem(i, kvs))

    barrier = pltpu.get_barrier_semaphore()

    def greet(step, _):
        pl.semaphore_signal(
            barrier, inc=1, device_id=device(lax.rem(me + step, n)), device_id_type=MESH
        )
        return 0

    lax.fori_loop(1, n, greet, 0)
    for i, fetch in enumerate(fetches):
        if i not in first_needed:
            fetch.start()
    for i in first_needed:
        fetches[i].wait()

    def spread(slot):
        pos_cols = (near_pos[slot] * (1.0 / (2.0 * math.pi))).T
        for d in range(3):
            posb[d] = jnp.broadcast_to(pos_cols[:, d : d + 1], (atoms, LANES))

    def fill_tile(slot, tile):
        cols = pl.ds(pl.multiple_of(tile * LANES, LANES), LANES)
        turns = (
            posb[0] * wave_ref[0:1, cols]
            + posb[1] * wave_ref[1:2, cols]
            + posb[2] * wave_ref[2:3, cols]
        )
        turns = turns - jnp.round(turns)
        square = turns * turns
        cos_tab[slot, :, cols] = horner(COS_TURN, square).astype(BF16)
        sin_tab[slot, :, cols] = (horner(SIN_TURN, square) * turns).astype(BF16)

    near_pos[0] = jnp.concatenate([pos_ref[...], jnp.zeros((5, atoms), F32)], axis=0)
    near_feat[0] = feat_ref[...]
    spread(0)

    kx, ky, kz = wave_ref[0:1, :], wave_ref[1:2, :], wave_ref[2:3, :]
    sq_norm = kx * kx + ky * ky + kz * kz
    weight = jnp.exp(-0.5 * sq_norm) / (sq_norm + 1.0)
    weight = weight * (LONG_SCALE / math.sqrt(waves) / math.sqrt(total_atoms))

    per = math.gcd(4, wave_tiles)
    turns_of = wave_tiles // per

    def send_structure(block, charge, fill):
        both = jnp.concatenate(halves(charge), axis=0)

        def some_tiles(step, _):
            start = lax.rem(step + me, turns_of) * per
            if fill:
                for i in range(per):
                    fill_tile(0, start + i)
            cols = pl.ds(pl.multiple_of(start * LANES, LANES), per * LANES)
            for half, tab in enumerate((cos_tab, sin_tab)):
                part = contract(both, tab[0, :, cols], 1, 0)
                part = (part[:chan] + part[chan:]).astype(BF16)
                for i in range(per):
                    owner = half * wave_tiles + start + i
                    send[block, owner] = part[:, i * LANES : (i + 1) * LANES]
            for half in range(2):
                for i in range(per):
                    owner = half * wave_tiles + start + i

                    @pl.when(owner != me)
                    def _():
                        pltpu.make_async_remote_copy(
                            src_ref=send.at[block, owner],
                            dst_ref=recv.at[block, lax.rem(owner - me + n, n) - 1],
                            send_sem=red_send_sem.at[block],
                            recv_sem=red_recv_sem.at[block],
                            device_id=device(owner),
                            device_id_type=MESH,
                        ).start()

            return 0

        lax.fori_loop(0, turns_of, some_tiles, 0)

    def wait_bytes(ref, sem):
        pltpu.make_async_copy(ref, ref, sem).wait()

    def reduce_and_send(block):
        def own():
            wait_bytes(recv.at[block], red_recv_sem.at[block])
            total = send[block, me].astype(F32)
            for step in range(n - 1):
                total = total + recv[block, step].astype(F32)
            result[block, me] = total.astype(BF16)

            def put(step, _):
                pltpu.make_async_remote_copy(
                    src_ref=result.at[block, me],
                    dst_ref=result.at[block, me],
                    send_sem=bc_send_sem.at[block],
                    recv_sem=bc_recv_sem.at[block],
                    device_id=device(lax.rem(me + step, n)),
                    device_id_type=MESH,
                ).start()
                return 0

            lax.fori_loop(1, n, put, 0)

        if n > chunks:
            pl.when(me < chunks)(own)
        else:
            own()

    def wait_sums(block):
        def own():
            wait_bytes(result.at[block, pl.ds(0, chunks - 1)], bc_recv_sem.at[block])

        if n > chunks:
            pl.when(me < chunks)(own)

            @pl.when(me >= chunks)
            def _():
                wait_bytes(result.at[block], bc_recv_sem.at[block])
        else:
            own()

    def finish_sends(block):
        def own():
            wait_bytes(send.at[block, pl.ds(0, chunks - 1)], red_send_sem.at[block])
            wait_bytes(recv.at[block], bc_send_sem.at[block])

        if n > chunks:
            pl.when(me < chunks)(own)

            @pl.when(me >= chunks)
            def _():
                wait_bytes(send.at[block], red_send_sem.at[block])
        else:
            own()

    def weighted(block):
        return [
            jnp.concatenate(
                [result[block, half * wave_tiles + tile] for tile in range(wave_tiles)], axis=1
            ).astype(F32)
            * weight
            for half in (0, 1)
        ]

    def project(cos_w, sin_w, charge):
        on_cos = jnp.concatenate([cos_w, -kx * sin_w, -ky * sin_w, -kz * sin_w], axis=0)
        on_sin = jnp.concatenate([sin_w, kx * cos_w, ky * cos_w, kz * cos_w], axis=0)
        out = contract(jnp.concatenate(halves(on_cos), axis=0), cos_tab[0], 1, 1)
        out = out + contract(jnp.concatenate(halves(on_sin), axis=0), sin_tab[0], 1, 1)
        rows = 4 * chan
        out = out[:rows] + out[rows:]
        force = [
            jnp.sum(charge * out[chan * (d + 1) : chan * (d + 2)], axis=0, keepdims=True)
            for d in range(3)
        ]
        return out[:chan], jnp.concatenate(force, axis=0)

    def potential(cos_w, sin_w, slot):
        out = contract(jnp.concatenate(halves(cos_w), axis=0), cos_tab[slot], 1, 1)
        out = out + contract(jnp.concatenate(halves(sin_w), axis=0), sin_tab[slot], 1, 1)
        return out[:chan] + out[chan:]

    def lift(pot, wl_ref):
        high, low = halves(pot)
        w_high, w_low = halves(wl_ref[...])
        return contract(
            jnp.concatenate([high, low, high], axis=0),
            jnp.concatenate([w_high, w_high, w_low], axis=0),
            0,
            0,
        )

    features = feat_ref[...]
    charge = contract(wc1_ref[...], features, 1, 1)
    pl.semaphore_wait(barrier, n - 1)

    def put_near(step, _):
        peer = device(my_dom * kvs + lax.rem(my_kv + step, kvs))
        for ref, send_sem, recv_sem in (
            (near_pos, pos_send_sem, pos_recv_sem),
            (near_feat, feat_send_sem, feat_recv_sem),
        ):
            pltpu.make_async_remote_copy(
                src_ref=ref.at[0],
                dst_ref=ref.at[kvs - step],
                send_sem=send_sem,
                recv_sem=recv_sem,
                device_id=peer,
                device_id_type=MESH,
            ).start()
        return 0

    lax.fori_loop(1, kvs, put_near, 0)
    send_structure(0, charge, True)
    for i, fetch in enumerate(fetches):
        if i not in first_needed:
            fetch.wait()

    dist_t = dist_ref[...]
    slot_row = lax.broadcasted_iota(jnp.int32, (slots, atoms), 0)
    envelope = 0.5 * (jnp.cos(math.pi * dist_t / 5.0) + 1.0)
    envelope = jnp.where(slot_row < cnt_ref[...], envelope, 0.0)
    centers = 0.5 + 4.5 / (radial - 1) * lax.broadcasted_iota(jnp.int32, (radial, atoms), 0).astype(
        F32
    )
    sharpness = ((radial - 1) / 4.5) ** 2
    group = 256 // radial
    for s in range(slots):
        away = dist_t[s : s + 1] - centers
        values = jnp.exp(-sharpness * (away * away)) * envelope[s : s + 1]
        basis[s // group, (s % group) * radial : (s % group + 1) * radial] = values.astype(BF16)
    column = lax.broadcasted_iota(jnp.int32, (radial, 256), 1)
    row = lax.broadcasted_iota(jnp.int32, (radial, 256), 0)
    repeat = jnp.where(lax.rem(column, radial) == row, 1.0, 0.0).astype(BF16)
    wide = contract(wf_ref[...].astype(BF16), repeat, 0, 0)
    member = lax.div(lax.broadcasted_iota(jnp.int32, (hid, 256), 1), radial)
    filt = jnp.concatenate(
        [jnp.where(member == s, wide, 0.0).astype(BF16) for s in range(group)], axis=0
    )

    def one_group(g, _):
        scale[pl.ds(g * group, group)] = contract(filt, basis[g], 1, 0).reshape(group, hid, atoms)
        return 0

    lax.fori_loop(0, slots // group, one_group, 0)
    index = idx_ref[...]
    high_row[...] = lax.div(index, atoms)
    low = lax.rem(index, atoms).astype(F32)
    for s in range(slots):
        low_rows[s] = jnp.broadcast_to(low[s : s + 1], (16, atoms)).astype(BF16)

    reduce_and_send(0)
    wait_bytes(near_pos.at[pl.ds(1, kvs - 1)], pos_recv_sem)
    wait_bytes(near_feat.at[pl.ds(1, kvs - 1)], feat_recv_sem)

    def near_tables(slot, _):
        spread(slot)

        def near_tile(tile, _):
            fill_tile(slot, tile)
            return 0

        return lax.fori_loop(0, wave_tiles, near_tile, 0)

    lax.fori_loop(1, kvs, near_tables, 0)

    wait_sums(0)
    cos_w, sin_w = weighted(0)

    def domain_values(slot, _):
        pot = potential(cos_w, sin_w, slot)
        hidden = (near_feat[slot].astype(F32) + silu(lift(pot, wl1_ref))).astype(BF16)
        near_hidden[slot] = hidden
        values = contract(wv_ref[...], hidden, 0, 1).astype(BF16)
        table[lax.rem(my_kv + slot, kvs)] = values
        return 0

    lax.fori_loop(0, kvs, domain_values, 0)
    own_rows = lax.broadcasted_iota(jnp.int32, (atoms, atoms), 0)
    copies = []
    for side, turn in ((0, 1), (1, doms - 1)):
        for way in range(halo_ways):
            wanted = halo_ref[side : side + 1, way * atoms : (way + 1) * atoms]
            total = jnp.zeros((hid, atoms), F32)
            for q in range(kvs):
                picks = jnp.where(own_rows + q * atoms == wanted, 1.0, 0.0).astype(BF16)
                total = total + contract(table[q], picks, 1, 0)
            halo_out[side, way] = total.astype(BF16)
        copy = pltpu.make_async_remote_copy(
            src_ref=halo_out.at[side],
            dst_ref=table.at[pl.ds(kvs + side * halo_ways, halo_ways)],
            send_sem=halo_send_sem.at[side],
            recv_sem=halo_recv_sem.at[side],
            device_id=device(lax.rem(my_dom + turn, doms) * kvs + my_kv),
            device_id_type=MESH,
        )
        copy.start()
        copies.append(copy)
    pot, force = project(cos_w, sin_w, charge)
    for copy in copies:
        copy.wait()

    ways = kvs + 2 * halo_ways
    row_ids = lax.broadcasted_iota(jnp.int32, (atoms, atoms), 0).astype(F32).astype(BF16)
    row_ids = row_ids.reshape(atoms // 16, 16, atoms)
    one, zero = jnp.ones((), BF16), jnp.zeros((), BF16)
    message[...] = jnp.zeros_like(message)
    together = 4

    def some_slots(step, _):
        total = message[...]
        for s in range(together):
            s = step * together + s
            picks = jnp.where(row_ids == low_rows[s][None], one, zero).reshape(atoms, atoms)
            picked = contract(table[...].reshape(ways * hid, atoms), picks, 1, 0)
            high = high_row[pl.ds(s, 1), :]
            value = picked[:hid]
            for way in range(1, ways):
                value = jnp.where(high == way, picked[way * hid : (way + 1) * hid], value)
            total = total + scale[s] * value
        message[...] = total
        return 0

    lax.fori_loop(0, slots // together, some_slots, 0)
    hidden = (near_hidden[0].astype(F32) + silu(message[...]).T).astype(BF16)

    charge = contract(wc2_ref[...], hidden, 1, 1)
    send_structure(1, charge, False)
    reduce_and_send(1)
    wait_sums(1)
    pot, force_second = project(*weighted(1), charge)
    out_ref[...] = (hidden.astype(F32) + silu(lift(pot, wl2_ref))).astype(BF16)
    force_ref[...] = force + force_second

    wait_bytes(near_pos.at[pl.ds(1, kvs - 1)], pos_send_sem)
    wait_bytes(near_feat.at[pl.ds(1, kvs - 1)], feat_send_sem)
    finish_sends(0)
    finish_sends(1)


def local(doms, kvs, *args):
    (positions, features, nbr_index, nbr_count, nbr_dist, halo_lists, wave_vectors) = args[:7]
    weights = args[7:]
    n = doms * kvs
    atoms, hid = features.shape
    waves = wave_vectors.shape[1]
    slots = nbr_index.shape[1]
    radial = weights[3].shape[0]
    halo = halo_lists.shape[2]
    chan = weights[0].shape[1]
    ways = kvs + 2 * (halo // atoms)
    chunks = 2 * waves // LANES
    sem = pltpu.SemaphoreType.DMA
    vmem = pl.BlockSpec(memory_space=pltpu.VMEM)
    operands = (
        positions,
        features,
        nbr_index.T,
        nbr_count.reshape(1, atoms),
        nbr_dist.T,
        halo_lists.reshape(2, halo),
        wave_vectors,
        weights[0].T,
        weights[1],
        weights[2],
        weights[3],
        weights[4].T,
        weights[5],
    )
    return tuple(
        pl.pallas_call(
            functools.partial(kernel, doms, kvs, n * atoms),
            out_shape=(
                jax.ShapeDtypeStruct((atoms, hid), BF16),
                jax.ShapeDtypeStruct((3, atoms), F32),
            ),
            in_specs=[pl.BlockSpec(memory_space=pltpu.HBM)] * 13,
            out_specs=(vmem, vmem),
            scratch_shapes=[
                pltpu.VMEM((3, atoms, LANES), F32),
                pltpu.VMEM((kvs, atoms, waves), BF16),
                pltpu.VMEM((kvs, atoms, waves), BF16),
                pltpu.VMEM((2, chunks, chan, LANES), BF16),
                pltpu.VMEM((2, n - 1, chan, LANES), BF16),
                pltpu.VMEM((2, chunks, chan, LANES), BF16),
                pltpu.VMEM((kvs, 8, atoms), F32),
                pltpu.VMEM((kvs, atoms, hid), BF16),
                pltpu.VMEM((kvs, atoms, hid), BF16),
                pltpu.VMEM((2, halo // atoms, hid, atoms), BF16),
                pltpu.VMEM((ways, hid, atoms), BF16),
                pltpu.VMEM((slots * radial // 256, 256, atoms), BF16),
                pltpu.VMEM((slots, hid, atoms), F32),
                pltpu.VMEM((slots, 16, atoms), BF16),
                pltpu.VMEM((slots, atoms), jnp.int32),
                pltpu.VMEM((hid, atoms), F32),
                sem((2,)),
                sem((2,)),
                sem((2,)),
                sem((2,)),
                sem,
                sem,
                sem,
                sem,
                sem((2,)),
                sem((2,)),
                sem((13,)),
                *(pltpu.VMEM(x.shape, x.dtype) for x in operands),
            ],
            compiler_params=pltpu.CompilerParams(
                collective_id=0, has_side_effects=True, vmem_limit_bytes=48 * 1024 * 1024
            ),
        )(*operands)
    )


def solution(mesh):
    return jax.shard_map(
        functools.partial(local, mesh.shape["dom"], mesh.shape["kv"]),
        mesh=mesh,
        in_specs=(
            P(None, ("dom", "kv")),
            P(("dom", "kv"), None),
            P(("dom", "kv"), None),
            P(("dom", "kv")),
            P(("dom", "kv"), None),
            P("dom", None, None),
            P(),
            P(),
            P(),
            P(),
            P(),
            P(),
            P(),
        ),
        out_specs=(P(("dom", "kv"), None), P(None, ("dom", "kv"))),
        check_vma=False,
    )
```

```python
import functools
import math

import jax
import jax.numpy as jnp
from jax import lax
from jax.experimental import pallas as pl
from jax.experimental.pallas import tpu as pltpu
from jax.sharding import PartitionSpec as P

MESH = pl.DeviceIdType.MESH
LONG_SCALE = 2.0
LANES = 128
F32 = jnp.float32
BF16 = jnp.bfloat16
SIN_TURN = (
    6.283185005187988,
    -41.341590881347656,
    81.59994506835938,
    -76.61447143554688,
    41.3428840637207,
    -12.471243858337402,
)
COS_TURN = (
    0.9999992251396179,
    -19.738981246948242,
    64.92865753173828,
    -85.27162170410156,
    58.79049301147461,
    -21.07110595703125,
)


def contract(a, b, dim_a, dim_b):
    return lax.dot_general(
        a, b, (((dim_a,), (dim_b,)), ((), ())), preferred_element_type=F32
    )


def halves(x):
    high = x.astype(BF16)
    return high, (x - high.astype(F32)).astype(BF16)


def horner(coefs, x):
    value = jnp.full_like(x, coefs[-1])
    for coef in coefs[-2::-1]:
        value = value * x + coef
    return value


def silu(x):
    return x / (1.0 + jnp.exp(-x))


def kernel(doms, kvs, total_atoms, *refs):
    hbm_refs, refs = refs[:13], refs[13:]
    body(doms, kvs, total_atoms, hbm_refs, *refs)


def body(
    doms,
    kvs,
    total_atoms,
    hbm_refs,
    out_ref,
    force_ref,
    posb,
    cos_tab,
    sin_tab,
    send,
    recv,
    result,
    near_pos,
    near_feat,
    near_hidden,
    halo_out,
    table,
    basis,
    scale,
    low_rows,
    high_row,
    message,
    red_send_sem,
    red_recv_sem,
    bc_send_sem,
    bc_recv_sem,
    pos_send_sem,
    pos_recv_sem,
    feat_send_sem,
    feat_recv_sem,
    halo_send_sem,
    halo_recv_sem,
    in_sem,
    *in_refs,
):
    (
        pos_ref,
        feat_ref,
        idx_ref,
        cnt_ref,
        dist_ref,
        halo_ref,
        wave_ref,
        wc1_ref,
        wl1_ref,
        wv_ref,
        wf_ref,
        wc2_ref,
        wl2_ref,
    ) = in_refs
    fetches = [
        pltpu.make_async_copy(source, target, in_sem.at[i])
        for i, (source, target) in enumerate(zip(hbm_refs, in_refs))
    ]
    first_needed = (0, 1, 6, 7)
    for i in first_needed:
        fetches[i].start()
    n = doms * kvs
    atoms, hid = feat_ref.shape
    waves = wave_ref.shape[1]
    chan = wc1_ref.shape[0]
    slots = idx_ref.shape[0]
    radial = wf_ref.shape[0]
    halo = halo_ref.shape[1]
    halo_ways = halo // atoms
    wave_tiles = waves // LANES
    chunks = 2 * wave_tiles
    my_dom = lax.axis_index("dom")
    my_kv = lax.axis_index("kv")
    me = my_dom * kvs + my_kv

    def device(i):
        return (lax.div(i, kvs), lax.rem(i, kvs))

    barrier = pltpu.get_barrier_semaphore()

    def greet(step, _):
        pl.semaphore_signal(
            barrier, inc=1, device_id=device(lax.rem(me + step, n)), device_id_type=MESH
        )
        return 0

    lax.fori_loop(1, n, greet, 0)
    for i, fetch in enumerate(fetches):
        if i not in first_needed:
            fetch.start()
    for i in first_needed:
        fetches[i].wait()

    def spread(slot):
        pos_cols = (near_pos[slot] * (1.0 / (2.0 * math.pi))).T
        for d in range(3):
            posb[d] = jnp.broadcast_to(pos_cols[:, d : d + 1], (atoms, LANES))

    def fill_tile(slot, tile):
        cols = pl.ds(pl.multiple_of(tile * LANES, LANES), LANES)
        turns = (
            posb[0] * wave_ref[0:1, cols]
            + posb[1] * wave_ref[1:2, cols]
            + posb[2] * wave_ref[2:3, cols]
        )
        turns = turns - jnp.round(turns)
        square = turns * turns
        cos_tab[slot, :, cols] = horner(COS_TURN, square).astype(BF16)
        sin_tab[slot, :, cols] = (horner(SIN_TURN, square) * turns).astype(BF16)

    near_pos[0] = jnp.concatenate([pos_ref[...], jnp.zeros((5, atoms), F32)], axis=0)
    near_feat[0] = feat_ref[...]
    spread(0)

    kx, ky, kz = wave_ref[0:1, :], wave_ref[1:2, :], wave_ref[2:3, :]
    sq_norm = kx * kx + ky * ky + kz * kz
    weight = jnp.exp(-0.5 * sq_norm) / (sq_norm + 1.0)
    weight = weight * (LONG_SCALE / math.sqrt(waves) / math.sqrt(total_atoms))

    per = math.gcd(4, wave_tiles)
    turns_of = wave_tiles // per

    def send_structure(block, charge, fill):
        both = jnp.concatenate(halves(charge), axis=0)

        def some_tiles(step, _):
            start = lax.rem(step + me, turns_of) * per
            if fill:
                for i in range(per):
                    fill_tile(0, start + i)
            cols = pl.ds(pl.multiple_of(start * LANES, LANES), per * LANES)
            for half, tab in enumerate((cos_tab, sin_tab)):
                part = contract(both, tab[0, :, cols], 1, 0)
                part = (part[:chan] + part[chan:]).astype(BF16)
                for i in range(per):
                    owner = half * wave_tiles + start + i
                    send[block, owner] = part[:, i * LANES : (i + 1) * LANES]
            for half in range(2):
                for i in range(per):
                    owner = half * wave_tiles + start + i

                    @pl.when(owner != me)
                    def _():
                        pltpu.make_async_remote_copy(
                            src_ref=send.at[block, owner],
                            dst_ref=recv.at[block, lax.rem(owner - me + n, n) - 1],
                            send_sem=red_send_sem.at[block],
                            recv_sem=red_recv_sem.at[block],
                            device_id=device(owner),
                            device_id_type=MESH,
                        ).start()

            return 0

        lax.fori_loop(0, turns_of, some_tiles, 0)

    def wait_bytes(ref, sem):
        pltpu.make_async_copy(ref, ref, sem).wait()

    def reduce_and_send(block):
        def own():
            wait_bytes(recv.at[block], red_recv_sem.at[block])
            total = send[block, me].astype(F32)
            for step in range(n - 1):
                total = total + recv[block, step].astype(F32)
            result[block, me] = total.astype(BF16)

            def put(step, _):
                pltpu.make_async_remote_copy(
                    src_ref=result.at[block, me],
                    dst_ref=result.at[block, me],
                    send_sem=bc_send_sem.at[block],
                    recv_sem=bc_recv_sem.at[block],
                    device_id=device(lax.rem(me + step, n)),
                    device_id_type=MESH,
                ).start()
                return 0

            lax.fori_loop(1, n, put, 0)

        if n > chunks:
            pl.when(me < chunks)(own)
        else:
            own()

    def wait_sums(block):
        def own():
            wait_bytes(result.at[block, pl.ds(0, chunks - 1)], bc_recv_sem.at[block])

        if n > chunks:
            pl.when(me < chunks)(own)

            @pl.when(me >= chunks)
            def _():
                wait_bytes(result.at[block], bc_recv_sem.at[block])
        else:
            own()

    def finish_sends(block):
        def own():
            wait_bytes(send.at[block, pl.ds(0, chunks - 1)], red_send_sem.at[block])
            wait_bytes(recv.at[block], bc_send_sem.at[block])

        if n > chunks:
            pl.when(me < chunks)(own)

            @pl.when(me >= chunks)
            def _():
                wait_bytes(send.at[block], red_send_sem.at[block])
        else:
            own()

    def weighted(block):
        return [
            jnp.concatenate(
                [result[block, half * wave_tiles + tile] for tile in range(wave_tiles)], axis=1
            ).astype(F32)
            * weight
            for half in (0, 1)
        ]

    def project(cos_w, sin_w, charge):
        on_cos = jnp.concatenate([cos_w, -kx * sin_w, -ky * sin_w, -kz * sin_w], axis=0)
        on_sin = jnp.concatenate([sin_w, kx * cos_w, ky * cos_w, kz * cos_w], axis=0)
        out = contract(cos_tab[0], jnp.concatenate(halves(on_cos), axis=0), 1, 1)
        out = out + contract(sin_tab[0], jnp.concatenate(halves(on_sin), axis=0), 1, 1)
        out = out.T
        rows = 4 * chan
        out = out[:rows] + out[rows:]
        force = [
            jnp.sum(charge * out[chan * (d + 1) : chan * (d + 2)], axis=0, keepdims=True)
            for d in range(3)
        ]
        return out[:chan], jnp.concatenate(force, axis=0)

    def potential(cos_w, sin_w, slot):
        pad = jnp.zeros((LANES - 2 * chan, waves), BF16)
        out = contract(cos_tab[slot], jnp.concatenate([*halves(cos_w), pad], axis=0), 1, 1)
        out = out + contract(sin_tab[slot], jnp.concatenate([*halves(sin_w), pad], axis=0), 1, 1)
        out = out.T
        return out[:chan] + out[chan : 2 * chan]

    def lift(pot, wl_ref):
        high, low = halves(pot)
        w_high, w_low = halves(wl_ref[...])
        return contract(
            jnp.concatenate([high, low, high], axis=0),
            jnp.concatenate([w_high, w_high, w_low], axis=0),
            0,
            0,
        )

    features = feat_ref[...]
    charge = contract(wc1_ref[...], features, 1, 1)
    pl.semaphore_wait(barrier, n - 1)

    def put_near(step, _):
        peer = device(my_dom * kvs + lax.rem(my_kv + step, kvs))
        for ref, send_sem, recv_sem in (
            (near_pos, pos_send_sem, pos_recv_sem),
            (near_feat, feat_send_sem, feat_recv_sem),
        ):
            pltpu.make_async_remote_copy(
                src_ref=ref.at[0],
                dst_ref=ref.at[kvs - step],
                send_sem=send_sem,
                recv_sem=recv_sem,
                device_id=peer,
                device_id_type=MESH,
            ).start()
        return 0

    lax.fori_loop(1, kvs, put_near, 0)
    send_structure(0, charge, True)
    for i, fetch in enumerate(fetches):
        if i not in first_needed:
            fetch.wait()

    dist_t = dist_ref[...]
    slot_row = lax.broadcasted_iota(jnp.int32, (slots, atoms), 0)
    envelope = 0.5 * (jnp.cos(math.pi * dist_t / 5.0) + 1.0)
    envelope = jnp.where(slot_row < cnt_ref[...], envelope, 0.0)
    centers = 0.5 + 4.5 / (radial - 1) * lax.broadcasted_iota(jnp.int32, (radial, atoms), 0).astype(
        F32
    )
    sharpness = ((radial - 1) / 4.5) ** 2
    group = 256 // radial
    for s in range(slots):
        away = dist_t[s : s + 1] - centers
        values = jnp.exp(-sharpness * (away * away)) * envelope[s : s + 1]
        basis[s // group, (s % group) * radial : (s % group + 1) * radial] = values.astype(BF16)
    column = lax.broadcasted_iota(jnp.int32, (radial, 256), 1)
    row = lax.broadcasted_iota(jnp.int32, (radial, 256), 0)
    repeat = jnp.where(lax.rem(column, radial) == row, 1.0, 0.0).astype(BF16)
    wide = contract(wf_ref[...].astype(BF16), repeat, 0, 0)
    member = lax.div(lax.broadcasted_iota(jnp.int32, (hid, 256), 1), radial)
    filt = jnp.concatenate(
        [jnp.where(member == s, wide, 0.0).astype(BF16) for s in range(group)], axis=0
    )

    def one_group(g, _):
        scale[pl.ds(g * group, group)] = contract(filt, basis[g], 1, 0).reshape(group, hid, atoms)
        return 0

    lax.fori_loop(0, slots // group, one_group, 0)
    index = idx_ref[...]
    high_row[...] = lax.div(index, atoms)
    low = lax.rem(index, atoms).astype(F32)
    for s in range(slots):
        low_rows[s] = jnp.broadcast_to(low[s : s + 1], (16, atoms)).astype(BF16)

    reduce_and_send(0)
    wait_bytes(near_pos.at[pl.ds(1, kvs - 1)], pos_recv_sem)
    wait_bytes(near_feat.at[pl.ds(1, kvs - 1)], feat_recv_sem)

    def near_tables(slot, _):
        spread(slot)

        def near_tile(tile, _):
            fill_tile(slot, tile)
            return 0

        return lax.fori_loop(0, wave_tiles, near_tile, 0)

    lax.fori_loop(1, kvs, near_tables, 0)

    wait_sums(0)
    cos_w, sin_w = weighted(0)

    def domain_values(slot, _):
        pot = potential(cos_w, sin_w, slot)
        hidden = (near_feat[slot].astype(F32) + silu(lift(pot, wl1_ref))).astype(BF16)
        near_hidden[slot] = hidden
        values = contract(wv_ref[...], hidden, 0, 1).astype(BF16)
        table[lax.rem(my_kv + slot, kvs)] = values
        return 0

    lax.fori_loop(0, kvs, domain_values, 0)
    own_rows = lax.broadcasted_iota(jnp.int32, (atoms, atoms), 0)
    copies = []
    for side, turn in ((0, 1), (1, doms - 1)):
        for way in range(halo_ways):
            wanted = halo_ref[side : side + 1, way * atoms : (way + 1) * atoms]
            total = jnp.zeros((hid, atoms), F32)
            for q in range(kvs):
                picks = jnp.where(own_rows + q * atoms == wanted, 1.0, 0.0).astype(BF16)
                total = total + contract(table[q], picks, 1, 0)
            halo_out[side, way] = total.astype(BF16)
        copy = pltpu.make_async_remote_copy(
            src_ref=halo_out.at[side],
            dst_ref=table.at[pl.ds(kvs + side * halo_ways, halo_ways)],
            send_sem=halo_send_sem.at[side],
            recv_sem=halo_recv_sem.at[side],
            device_id=device(lax.rem(my_dom + turn, doms) * kvs + my_kv),
            device_id_type=MESH,
        )
        copy.start()
        copies.append(copy)
    pot, force = project(cos_w, sin_w, charge)
    for copy in copies:
        copy.wait()

    ways = kvs + 2 * halo_ways
    row_ids = lax.broadcasted_iota(jnp.int32, (atoms, atoms), 0).astype(F32).astype(BF16)
    row_ids = row_ids.reshape(atoms // 16, 16, atoms)
    one, zero = jnp.ones((), BF16), jnp.zeros((), BF16)
    message[...] = jnp.zeros_like(message)
    together = 4

    def some_slots(step, _):
        total = message[...]
        for s in range(together):
            s = step * together + s
            picks = jnp.where(row_ids == low_rows[s][None], one, zero).reshape(atoms, atoms)
            picked = contract(table[...].reshape(ways * hid, atoms), picks, 1, 0)
            high = high_row[pl.ds(s, 1), :]
            value = picked[:hid]
            for way in range(1, ways):
                value = jnp.where(high == way, picked[way * hid : (way + 1) * hid], value)
            total = total + scale[s] * value
        message[...] = total
        return 0

    lax.fori_loop(0, slots // together, some_slots, 0)
    hidden = (near_hidden[0].astype(F32) + silu(message[...]).T).astype(BF16)

    charge = contract(wc2_ref[...], hidden, 1, 1)
    send_structure(1, charge, False)
    reduce_and_send(1)
    wait_sums(1)
    pot, force_second = project(*weighted(1), charge)
    out_ref[...] = (hidden.astype(F32) + silu(lift(pot, wl2_ref))).astype(BF16)
    force_ref[...] = force + force_second

    wait_bytes(near_pos.at[pl.ds(1, kvs - 1)], pos_send_sem)
    wait_bytes(near_feat.at[pl.ds(1, kvs - 1)], feat_send_sem)
    finish_sends(0)
    finish_sends(1)


def local(doms, kvs, *args):
    (positions, features, nbr_index, nbr_count, nbr_dist, halo_lists, wave_vectors) = args[:7]
    weights = args[7:]
    n = doms * kvs
    atoms, hid = features.shape
    waves = wave_vectors.shape[1]
    slots = nbr_index.shape[1]
    radial = weights[3].shape[0]
    halo = halo_lists.shape[2]
    chan = weights[0].shape[1]
    ways = kvs + 2 * (halo // atoms)
    chunks = 2 * waves // LANES
    sem = pltpu.SemaphoreType.DMA
    vmem = pl.BlockSpec(memory_space=pltpu.VMEM)
    operands = (
        positions,
        features,
        nbr_index.T,
        nbr_count.reshape(1, atoms),
        nbr_dist.T,
        halo_lists.reshape(2, halo),
        wave_vectors,
        weights[0].T,
        weights[1],
        weights[2],
        weights[3],
        weights[4].T,
        weights[5],
    )
    return tuple(
        pl.pallas_call(
            functools.partial(kernel, doms, kvs, n * atoms),
            out_shape=(
                jax.ShapeDtypeStruct((atoms, hid), BF16),
                jax.ShapeDtypeStruct((3, atoms), F32),
            ),
            in_specs=[pl.BlockSpec(memory_space=pltpu.HBM)] * 13,
            out_specs=(vmem, vmem),
            scratch_shapes=[
                pltpu.VMEM((3, atoms, LANES), F32),
                pltpu.VMEM((kvs, atoms, waves), BF16),
                pltpu.VMEM((kvs, atoms, waves), BF16),
                pltpu.VMEM((2, chunks, chan, LANES), BF16),
                pltpu.VMEM((2, n - 1, chan, LANES), BF16),
                pltpu.VMEM((2, chunks, chan, LANES), BF16),
                pltpu.VMEM((kvs, 8, atoms), F32),
                pltpu.VMEM((kvs, atoms, hid), BF16),
                pltpu.VMEM((kvs, atoms, hid), BF16),
                pltpu.VMEM((2, halo // atoms, hid, atoms), BF16),
                pltpu.VMEM((ways, hid, atoms), BF16),
                pltpu.VMEM((slots * radial // 256, 256, atoms), BF16),
                pltpu.VMEM((slots, hid, atoms), F32),
                pltpu.VMEM((slots, 16, atoms), BF16),
                pltpu.VMEM((slots, atoms), jnp.int32),
                pltpu.VMEM((hid, atoms), F32),
                sem((2,)),
                sem((2,)),
                sem((2,)),
                sem((2,)),
                sem,
                sem,
                sem,
                sem,
                sem((2,)),
                sem((2,)),
                sem((13,)),
                *(pltpu.VMEM(x.shape, x.dtype) for x in operands),
            ],
            compiler_params=pltpu.CompilerParams(
                collective_id=0, has_side_effects=True, vmem_limit_bytes=64 * 1024 * 1024
            ),
        )(*operands)
    )


def solution(mesh):
    return jax.shard_map(
        functools.partial(local, mesh.shape["dom"], mesh.shape["kv"]),
        mesh=mesh,
        in_specs=(
            P(None, ("dom", "kv")),
            P(("dom", "kv"), None),
            P(("dom", "kv"), None),
            P(("dom", "kv")),
            P(("dom", "kv"), None),
            P("dom", None, None),
            P(),
            P(),
            P(),
            P(),
            P(),
            P(),
            P(),
        ),
        out_specs=(P(("dom", "kv"), None), P(None, ("dom", "kv"))),
        check_vma=False,
    )
```

```python
import functools
import math

import jax
import jax.numpy as jnp
from jax import lax
from jax.experimental import pallas as pl
from jax.experimental.pallas import tpu as pltpu
from jax.sharding import PartitionSpec as P

MESH = pl.DeviceIdType.MESH
LONG_SCALE = 2.0
LANES = 128
F32 = jnp.float32
BF16 = jnp.bfloat16
SIN_TURN = (
    6.283185005187988,
    -41.341590881347656,
    81.59994506835938,
    -76.61447143554688,
    41.3428840637207,
    -12.471243858337402,
)
COS_TURN = (
    0.9999992251396179,
    -19.738981246948242,
    64.92865753173828,
    -85.27162170410156,
    58.79049301147461,
    -21.07110595703125,
)


def contract(a, b, dim_a, dim_b):
    return lax.dot_general(
        a, b, (((dim_a,), (dim_b,)), ((), ())), preferred_element_type=F32
    )


def halves(x):
    high = x.astype(BF16)
    return high, (x - high.astype(F32)).astype(BF16)


def horner(coefs, x):
    value = jnp.full_like(x, coefs[-1])
    for coef in coefs[-2::-1]:
        value = value * x + coef
    return value


def silu(x):
    return x / (1.0 + jnp.exp(-x))


def kernel(doms, kvs, total_atoms, *refs):
    hbm_refs, refs = refs[:13], refs[13:]
    body(doms, kvs, total_atoms, hbm_refs, *refs)


def body(
    doms,
    kvs,
    total_atoms,
    hbm_refs,
    out_ref,
    force_ref,
    posb,
    cos_tab,
    sin_tab,
    send,
    recv,
    result,
    near_pos,
    near_feat,
    near_hidden,
    halo_out,
    table,
    basis,
    scale,
    low_rows,
    high_row,
    message,
    red_send_sem,
    red_recv_sem,
    bc_send_sem,
    bc_recv_sem,
    pos_send_sem,
    pos_recv_sem,
    feat_send_sem,
    feat_recv_sem,
    halo_send_sem,
    halo_recv_sem,
    in_sem,
    *in_refs,
):
    (
        pos_ref,
        feat_ref,
        idx_ref,
        cnt_ref,
        dist_ref,
        halo_ref,
        wave_ref,
        wc1_ref,
        wl1_ref,
        wv_ref,
        wf_ref,
        wc2_ref,
        wl2_ref,
    ) = in_refs
    fetches = [
        pltpu.make_async_copy(source, target, in_sem.at[i])
        for i, (source, target) in enumerate(zip(hbm_refs, in_refs))
    ]
    first_needed = (0, 1, 6, 7)
    for i in first_needed:
        fetches[i].start()
    n = doms * kvs
    atoms, hid = feat_ref.shape
    waves = wave_ref.shape[1]
    chan = wc1_ref.shape[0]
    slots = idx_ref.shape[0]
    radial = wf_ref.shape[0]
    halo = halo_ref.shape[1]
    halo_ways = halo // atoms
    wave_tiles = waves // LANES
    chunks = 2 * wave_tiles
    my_dom = lax.axis_index("dom")
    my_kv = lax.axis_index("kv")
    me = my_dom * kvs + my_kv

    def device(i):
        return (lax.div(i, kvs), lax.rem(i, kvs))

    barrier = pltpu.get_barrier_semaphore()

    def greet(step, _):
        pl.semaphore_signal(
            barrier, inc=1, device_id=device(lax.rem(me + step, n)), device_id_type=MESH
        )
        return 0

    lax.fori_loop(1, n, greet, 0)
    for i, fetch in enumerate(fetches):
        if i not in first_needed:
            fetch.start()
    for i in first_needed:
        fetches[i].wait()

    def spread(slot):
        pos_cols = (near_pos[slot] * (1.0 / (2.0 * math.pi))).T
        for d in range(3):
            posb[d] = jnp.broadcast_to(pos_cols[:, d : d + 1], (atoms, LANES))

    def fill_tile(slot, tile):
        cols = pl.ds(pl.multiple_of(tile * LANES, LANES), LANES)
        turns = (
            posb[0] * wave_ref[0:1, cols]
            + posb[1] * wave_ref[1:2, cols]
            + posb[2] * wave_ref[2:3, cols]
        )
        turns = turns - jnp.round(turns)
        square = turns * turns
        cos_tab[slot, :, cols] = horner(COS_TURN, square).astype(BF16)
        sin_tab[slot, :, cols] = (horner(SIN_TURN, square) * turns).astype(BF16)

    near_pos[0] = jnp.concatenate([pos_ref[...], jnp.zeros((5, atoms), F32)], axis=0)
    near_feat[0] = feat_ref[...]
    spread(0)

    kx, ky, kz = wave_ref[0:1, :], wave_ref[1:2, :], wave_ref[2:3, :]
    sq_norm = kx * kx + ky * ky + kz * kz
    weight = jnp.exp(-0.5 * sq_norm) / (sq_norm + 1.0)
    weight = weight * (LONG_SCALE / math.sqrt(waves) / math.sqrt(total_atoms))

    per = math.gcd(4, wave_tiles)
    turns_of = wave_tiles // per

    def send_structure(block, charge, fill):
        both = jnp.concatenate(halves(charge), axis=0)

        def some_tiles(step, _):
            start = lax.rem(step + me, turns_of) * per
            if fill:
                for i in range(per):
                    fill_tile(0, start + i)
            cols = pl.ds(pl.multiple_of(start * LANES, LANES), per * LANES)
            for half, tab in enumerate((cos_tab, sin_tab)):
                part = contract(both, tab[0, :, cols], 1, 0)
                part = (part[:chan] + part[chan:]).astype(BF16)
                for i in range(per):
                    owner = half * wave_tiles + start + i
                    send[block, owner] = part[:, i * LANES : (i + 1) * LANES]
            for half in range(2):
                for i in range(per):
                    owner = half * wave_tiles + start + i

                    @pl.when(owner != me)
                    def _():
                        pltpu.make_async_remote_copy(
                            src_ref=send.at[block, owner],
                            dst_ref=recv.at[block, lax.rem(owner - me + n, n) - 1],
                            send_sem=red_send_sem.at[block],
                            recv_sem=red_recv_sem.at[block],
                            device_id=device(owner),
                            device_id_type=MESH,
                        ).start()

            return 0

        lax.fori_loop(0, turns_of, some_tiles, 0)

    def wait_bytes(ref, sem):
        pltpu.make_async_copy(ref, ref, sem).wait()

    def reduce_and_send(block):
        def own():
            wait_bytes(recv.at[block], red_recv_sem.at[block])
            total = send[block, me].astype(F32)
            for step in range(n - 1):
                total = total + recv[block, step].astype(F32)
            result[block, me] = total.astype(BF16)

            def put(step, _):
                pltpu.make_async_remote_copy(
                    src_ref=result.at[block, me],
                    dst_ref=result.at[block, me],
                    send_sem=bc_send_sem.at[block],
                    recv_sem=bc_recv_sem.at[block],
                    device_id=device(lax.rem(me + step, n)),
                    device_id_type=MESH,
                ).start()
                return 0

            lax.fori_loop(1, n, put, 0)

        if n > chunks:
            pl.when(me < chunks)(own)
        else:
            own()

    def wait_sums(block):
        def own():
            wait_bytes(result.at[block, pl.ds(0, chunks - 1)], bc_recv_sem.at[block])

        if n > chunks:
            pl.when(me < chunks)(own)

            @pl.when(me >= chunks)
            def _():
                wait_bytes(result.at[block], bc_recv_sem.at[block])
        else:
            own()

    def finish_sends(block):
        def own():
            wait_bytes(send.at[block, pl.ds(0, chunks - 1)], red_send_sem.at[block])
            wait_bytes(recv.at[block], bc_send_sem.at[block])

        if n > chunks:
            pl.when(me < chunks)(own)

            @pl.when(me >= chunks)
            def _():
                wait_bytes(send.at[block], red_send_sem.at[block])
        else:
            own()

    def weighted(block):
        return [
            jnp.concatenate(
                [result[block, half * wave_tiles + tile] for tile in range(wave_tiles)], axis=1
            ).astype(F32)
            * weight
            for half in (0, 1)
        ]

    def project(cos_w, sin_w, charge):
        on_cos = jnp.concatenate([cos_w, -kx * sin_w, -ky * sin_w, -kz * sin_w], axis=0)
        on_sin = jnp.concatenate([sin_w, kx * cos_w, ky * cos_w, kz * cos_w], axis=0)
        out = contract(cos_tab[0], jnp.concatenate(halves(on_cos), axis=0), 1, 1)
        out = out + contract(sin_tab[0], jnp.concatenate(halves(on_sin), axis=0), 1, 1)
        out = out.T
        rows = 4 * chan
        out = out[:rows] + out[rows:]
        force = [
            jnp.sum(charge * out[chan * (d + 1) : chan * (d + 2)], axis=0, keepdims=True)
            for d in range(3)
        ]
        return out[:chan], jnp.concatenate(force, axis=0)

    def potential(cos_w, sin_w, slot):
        pad = jnp.zeros((LANES - 2 * chan, waves), BF16)
        out = contract(cos_tab[slot], jnp.concatenate([*halves(cos_w), pad], axis=0), 1, 1)
        out = out + contract(sin_tab[slot], jnp.concatenate([*halves(sin_w), pad], axis=0), 1, 1)
        out = out.T
        return out[:chan] + out[chan : 2 * chan]

    def lift(pot, wl_ref):
        high, low = halves(pot)
        w_high, w_low = halves(wl_ref[...])
        return contract(
            jnp.concatenate([high, low, high], axis=0),
            jnp.concatenate([w_high, w_high, w_low], axis=0),
            0,
            0,
        )

    features = feat_ref[...]
    charge = contract(wc1_ref[...], features, 1, 1)
    pl.semaphore_wait(barrier, n - 1)

    def put_near(step, _):
        peer = device(my_dom * kvs + lax.rem(my_kv + step, kvs))
        for ref, send_sem, recv_sem in (
            (near_pos, pos_send_sem, pos_recv_sem),
            (near_feat, feat_send_sem, feat_recv_sem),
        ):
            pltpu.make_async_remote_copy(
                src_ref=ref.at[0],
                dst_ref=ref.at[kvs - step],
                send_sem=send_sem,
                recv_sem=recv_sem,
                device_id=peer,
                device_id_type=MESH,
            ).start()
        return 0

    lax.fori_loop(1, kvs, put_near, 0)
    send_structure(0, charge, True)
    for i, fetch in enumerate(fetches):
        if i not in first_needed:
            fetch.wait()

    dist_t = dist_ref[...]
    slot_row = lax.broadcasted_iota(jnp.int32, (slots, atoms), 0)
    envelope = 0.5 * (jnp.cos(math.pi * dist_t / 5.0) + 1.0)
    envelope = jnp.where(slot_row < cnt_ref[...], envelope, 0.0)
    centers = 0.5 + 4.5 / (radial - 1) * lax.broadcasted_iota(jnp.int32, (radial, atoms), 0).astype(
        F32
    )
    sharpness = ((radial - 1) / 4.5) ** 2
    group = 256 // radial
    for s in range(slots):
        away = dist_t[s : s + 1] - centers
        values = jnp.exp(-sharpness * (away * away)) * envelope[s : s + 1]
        basis[s // group, (s % group) * radial : (s % group + 1) * radial] = values.astype(BF16)
    column = lax.broadcasted_iota(jnp.int32, (radial, 256), 1)
    row = lax.broadcasted_iota(jnp.int32, (radial, 256), 0)
    repeat = jnp.where(lax.rem(column, radial) == row, 1.0, 0.0).astype(BF16)
    wide = contract(wf_ref[...].astype(BF16), repeat, 0, 0)
    member = lax.div(lax.broadcasted_iota(jnp.int32, (hid, 256), 1), radial)
    filt = jnp.concatenate(
        [jnp.where(member == s, wide, 0.0).astype(BF16) for s in range(group)], axis=0
    )

    def one_group(g, _):
        scale[pl.ds(g * group, group)] = contract(filt, basis[g], 1, 0).reshape(group, hid, atoms)
        return 0

    lax.fori_loop(0, slots // group, one_group, 0)
    index = idx_ref[...]
    high_row[...] = lax.div(index, atoms)
    low = lax.rem(index, atoms).astype(F32)
    for s in range(slots):
        low_rows[s] = jnp.broadcast_to(low[s : s + 1], (16, atoms)).astype(BF16)

    reduce_and_send(0)
    wait_bytes(near_pos.at[pl.ds(1, kvs - 1)], pos_recv_sem)
    wait_bytes(near_feat.at[pl.ds(1, kvs - 1)], feat_recv_sem)

    def near_tables(slot, _):
        spread(slot)

        def near_tile(tile, _):
            fill_tile(slot, tile)
            return 0

        return lax.fori_loop(0, wave_tiles, near_tile, 0)

    lax.fori_loop(1, kvs, near_tables, 0)

    wait_sums(0)
    cos_w, sin_w = weighted(0)

    def domain_values(slot, _):
        pot = potential(cos_w, sin_w, slot)
        hidden = (near_feat[slot].astype(F32) + silu(lift(pot, wl1_ref))).astype(BF16)
        near_hidden[slot] = hidden
        values = contract(wv_ref[...], hidden, 0, 1).astype(BF16)
        table[lax.rem(my_kv + slot, kvs)] = values
        return 0

    lax.fori_loop(0, kvs, domain_values, 0)
    own_rows = lax.broadcasted_iota(jnp.int32, (atoms, atoms), 0)
    copies = []
    for side, turn in ((0, 1), (1, doms - 1)):
        for way in range(halo_ways):
            wanted = halo_ref[side : side + 1, way * atoms : (way + 1) * atoms]
            total = jnp.zeros((hid, atoms), F32)
            for q in range(kvs):
                picks = jnp.where(own_rows + q * atoms == wanted, 1.0, 0.0).astype(BF16)
                total = total + contract(table[q], picks, 1, 0)
            halo_out[side, way] = total.astype(BF16)
        copy = pltpu.make_async_remote_copy(
            src_ref=halo_out.at[side],
            dst_ref=table.at[pl.ds(kvs + side * halo_ways, halo_ways)],
            send_sem=halo_send_sem.at[side],
            recv_sem=halo_recv_sem.at[side],
            device_id=device(lax.rem(my_dom + turn, doms) * kvs + my_kv),
            device_id_type=MESH,
        )
        copy.start()
        copies.append(copy)
    pot, force = project(cos_w, sin_w, charge)
    for copy in copies:
        copy.wait()

    ways = kvs + 2 * halo_ways
    row_ids = lax.broadcasted_iota(jnp.int32, (atoms, atoms), 0).astype(F32).astype(BF16)
    row_ids = row_ids.reshape(atoms // 16, 16, atoms)
    one, zero = jnp.ones((), BF16), jnp.zeros((), BF16)
    message[...] = jnp.zeros_like(message)
    together = 8

    def some_slots(step, _):
        total = message[...]
        for s in range(together):
            s = step * together + s
            picks = jnp.where(row_ids == low_rows[s][None], one, zero).reshape(atoms, atoms)
            picked = contract(table[...].reshape(ways * hid, atoms), picks, 1, 0)
            high = high_row[pl.ds(s, 1), :]
            value = picked[:hid]
            for way in range(1, ways):
                value = jnp.where(high == way, picked[way * hid : (way + 1) * hid], value)
            total = total + scale[s] * value
        message[...] = total
        return 0

    lax.fori_loop(0, slots // together, some_slots, 0)
    hidden = (near_hidden[0].astype(F32) + silu(message[...]).T).astype(BF16)

    charge = contract(wc2_ref[...], hidden, 1, 1)
    send_structure(1, charge, False)
    reduce_and_send(1)
    wait_sums(1)
    pot, force_second = project(*weighted(1), charge)
    out_ref[...] = hidden.astype(F32) + silu(lift(pot, wl2_ref))
    force_ref[...] = force + force_second

    wait_bytes(near_pos.at[pl.ds(1, kvs - 1)], pos_send_sem)
    wait_bytes(near_feat.at[pl.ds(1, kvs - 1)], feat_send_sem)
    finish_sends(0)
    finish_sends(1)


def local(doms, kvs, *args):
    (positions, features, nbr_index, nbr_count, nbr_dist, halo_lists, wave_vectors) = args[:7]
    weights = args[7:]
    n = doms * kvs
    atoms, hid = features.shape
    waves = wave_vectors.shape[1]
    slots = nbr_index.shape[1]
    radial = weights[3].shape[0]
    halo = halo_lists.shape[2]
    chan = weights[0].shape[1]
    ways = kvs + 2 * (halo // atoms)
    chunks = 2 * waves // LANES
    sem = pltpu.SemaphoreType.DMA
    vmem = pl.BlockSpec(memory_space=pltpu.VMEM)
    operands = (
        positions,
        features,
        nbr_index.T,
        nbr_count.reshape(1, atoms),
        nbr_dist.T,
        halo_lists.reshape(2, halo),
        wave_vectors,
        weights[0].T,
        weights[1],
        weights[2],
        weights[3],
        weights[4].T,
        weights[5],
    )
    out, forces = (
        pl.pallas_call(
            functools.partial(kernel, doms, kvs, n * atoms),
            out_shape=(
                jax.ShapeDtypeStruct((atoms, hid), F32),
                jax.ShapeDtypeStruct((3, atoms), F32),
            ),
            in_specs=[pl.BlockSpec(memory_space=pltpu.HBM)] * 13,
            out_specs=(vmem, vmem),
            scratch_shapes=[
                pltpu.VMEM((3, atoms, LANES), F32),
                pltpu.VMEM((kvs, atoms, waves), BF16),
                pltpu.VMEM((kvs, atoms, waves), BF16),
                pltpu.VMEM((2, chunks, chan, LANES), BF16),
                pltpu.VMEM((2, n - 1, chan, LANES), BF16),
                pltpu.VMEM((2, chunks, chan, LANES), BF16),
                pltpu.VMEM((kvs, 8, atoms), F32),
                pltpu.VMEM((kvs, atoms, hid), BF16),
                pltpu.VMEM((kvs, atoms, hid), BF16),
                pltpu.VMEM((2, halo // atoms, hid, atoms), BF16),
                pltpu.VMEM((ways, hid, atoms), BF16),
                pltpu.VMEM((slots * radial // 256, 256, atoms), BF16),
                pltpu.VMEM((slots, hid, atoms), F32),
                pltpu.VMEM((slots, 16, atoms), BF16),
                pltpu.VMEM((slots, atoms), jnp.int32),
                pltpu.VMEM((hid, atoms), F32),
                sem((2,)),
                sem((2,)),
                sem((2,)),
                sem((2,)),
                sem,
                sem,
                sem,
                sem,
                sem((2,)),
                sem((2,)),
                sem((13,)),
                *(pltpu.VMEM(x.shape, x.dtype) for x in operands),
            ],
            compiler_params=pltpu.CompilerParams(
                collective_id=0, has_side_effects=True, vmem_limit_bytes=64 * 1024 * 1024
            ),
        )(*operands)
    )
    return out.astype(BF16), forces


def solution(mesh):
    return jax.shard_map(
        functools.partial(local, mesh.shape["dom"], mesh.shape["kv"]),
        mesh=mesh,
        in_specs=(
            P(None, ("dom", "kv")),
            P(("dom", "kv"), None),
            P(("dom", "kv"), None),
            P(("dom", "kv")),
            P(("dom", "kv"), None),
            P("dom", None, None),
            P(),
            P(),
            P(),
            P(),
            P(),
            P(),
            P(),
        ),
        out_specs=(P(("dom", "kv"), None), P(None, ("dom", "kv"))),
        check_vma=False,
    )
```
